256 devices in a mesh: dp: 16 (over z_hi, y, core), ctx: 16 (over x, z_lo).
Axes of the slice: x: 4, y: 4, z: 8 (z_hi: 2, z_lo: 4; z = z_hi * 4 + z_lo), core: 2. Of those that a mesh axis runs over, the one named last changes fastest.
Arguments:
- query_nope: bfloat16 [16, 2048, 2048], P('dp', 'ctx'), may hold values from -6 to 6
- query_rope: bfloat16 [16, 2048, 1024], P('dp', 'ctx'), may hold values from -9 to 9
- latent: bfloat16 [16, 2048, 512], P('dp', 'ctx'), may hold values from -6 to 6
- key_rope: bfloat16 [16, 2048, 64], P('dp', 'ctx'), may hold values from -6 to 6
- grad_output: bfloat16 [16, 2048, 2048], P('dp', 'ctx'), may hold values from -6 to 6
- kv_up: bfloat16 [512, 4096], replicated, may hold values from -0.25 to 0.25
- doc_lengths: int32 [16, 8], P('dp'), may hold values from 1 to 1536, 2048 in all within a row
Outputs:
- grad_query_nope: bfloat16 [16, 2048, 2048], P('dp', 'ctx')
- grad_query_rope: bfloat16 [16, 2048, 1024], P('dp', 'ctx')
- grad_latent: bfloat16 [16, 2048, 512], P('dp', 'ctx')
- grad_key_rope: bfloat16 [16, 2048, 64], P('dp', 'ctx')
- grad_kv_up: float32 [512, 4096], P('ctx')
The draws below stay inside these ranges and needn't reach their ends.
All inputs are finite; a program needn't handle non-finite values.
Results may differ from the reference program's by a relative error of at most 0.015.
Values may be sent and summed in bfloat16 or wider, within the bound.
A program may use at most 128 MiB of HBM per device.

```python
import math
import jax
import jax.numpy as jnp
import numpy as np
from jax import lax

HEAD_COUNT = 16
HEAD_DIM = 128
VALUE_DIM = 128
ROPE_DIM = 64
LATENT = 512
DOC_COUNT = 8
SEQ_LEN = 2048
SEQ_COUNT = 16


def draw_key_rope(key, part):
    key = jax.random.fold_in(key, 11)
    values = jnp.clip(jax.random.normal(key, (SEQ_COUNT, SEQ_LEN, ROPE_DIM), jnp.float32), -4.0, 4.0)
    return values.astype(jnp.bfloat16)


def draw_query_rope(key, part):
    key = jax.random.fold_in(key, 12)
    values = jnp.clip(jax.random.normal(key, (SEQ_COUNT, SEQ_LEN, HEAD_COUNT * ROPE_DIM), jnp.float32), -4.0, 4.0)
    return values.astype(jnp.bfloat16)


def steps_of(rng, shape, pieces, low, top_value):
    factor_of = 1.0
    for axis_at, parts in pieces:
        steps = jax.random.uniform(jax.random.fold_in(jax.random.fold_in(rng, 6), axis_at), (parts,), jnp.float32, low / len(pieces), top_value / len(pieces))
        factor_of = factor_of * jnp.repeat(jnp.exp(steps), shape[axis_at] // parts).reshape((-1,) + (1,) * (len(shape) - 1 - axis_at))
    return factor_of


def profile(amount, total, bound, slope):
    weights = [(1 << 20) // math.isqrt(grade ** slope) + 1 for grade in range(2, amount + 1)]
    surplus, given = total - bound - (amount - 1), [1] * (amount - 1)
    while surplus > 0:
        free = [i for i in range(amount - 1) if given[i] < bound]
        mass, left = sum([weights[i] for i in free]), surplus
        for i in free:
            more = min(bound - given[i], max(1, left * weights[i] // mass), surplus)
            given[i] = given[i] + more
            surplus = surplus - more
    return np.array([bound] + given)


def uneven_parts(key, amount, total, bound, skew):
    if amount == 2:
        one = jax.random.randint(key, (), max(1, total - bound), min(bound, total - 1) + 1)
        return jnp.stack([one, total - one])
    sizes = jnp.asarray(profile(amount, total, bound, skew), jnp.int32)
    pairs = (amount - 1) // 2
    giver, sink = sizes[1:1 + 2 * pairs:2], sizes[2:2 + 2 * pairs:2]
    slack = jnp.minimum(giver - 1, bound - sink)
    shifted = jax.random.randint(jax.random.fold_in(key, 1), (pairs,), 0, 1 << 20) % (slack + 1)
    sizes = sizes.at[1:1 + 2 * pairs:2].set(giver - shifted).at[2:2 + 2 * pairs:2].set(sink + shifted)
    return sizes[jax.random.permutation(jax.random.fold_in(key, 2), amount)]


def scatter_about(rng, dims, scale, bound, cuts=(), kind=jnp.bfloat16):
    values = jax.random.normal(rng, dims, jnp.float32) * scale
    if len(cuts) > 0:
        values = steps_of(rng, dims, cuts, -0.22, 0.18) * values
    return jnp.clip(values, min=-bound, max=bound).astype(kind)


def setup_inputs(seed: int = 0) -> dict:
    keys = jax.random.split(jax.random.key(seed), 8)
    return {
        "query_nope": scatter_about(keys[0], (SEQ_COUNT, SEQ_LEN, HEAD_COUNT * HEAD_DIM), 1.0, 6.0, ((0, 16), (1, 16))),
        "query_rope": draw_query_rope(jax.random.fold_in(keys[7], 71), 0),
        "latent": scatter_about(keys[2], (SEQ_COUNT, SEQ_LEN, LATENT), 1.0, 6.0, ((0, 16), (1, 16))),
        "key_rope": draw_key_rope(jax.random.fold_in(keys[7], 71), 0),
        "grad_output": scatter_about(keys[4], (SEQ_COUNT, SEQ_LEN, HEAD_COUNT * VALUE_DIM), 1.0, 6.0, ((0, 16), (1, 16))),
        "kv_up": scatter_about(keys[5], (LATENT, HEAD_COUNT * (HEAD_DIM + VALUE_DIM)), LATENT ** -0.5, 0.25),
        "doc_lengths": jax.vmap(lambda own: uneven_parts(own, DOC_COUNT, SEQ_LEN, SEQ_LEN // 2 + SEQ_LEN // 4, 2))(jax.random.split(keys[6], SEQ_COUNT)).reshape((SEQ_COUNT, DOC_COUNT)).astype(jnp.int32),
    }


NEGATIVE = -1e30


def product(form, left, right):
    return jnp.einsum(form, left.astype(jnp.float32), right.astype(jnp.float32))


def doc_bounds(lengths, positions):
    doc_ends = jnp.cumsum(lengths).astype(jnp.int32)
    before = doc_ends[None, :] <= positions[:, None]
    doc_ident = jnp.sum(before.astype(jnp.int32), axis=1).astype(jnp.int32)
    doc_first = jnp.max(jnp.where(before, doc_ends[None, :], 0), axis=1).astype(jnp.int32)
    return doc_ident, doc_first


def visible_block(query_pos, query_doc, key_first, extent, lengths):
    key_pos = key_first + jnp.arange(extent, dtype=jnp.int32)
    key_doc, unused_first = doc_bounds(lengths, key_pos)
    return (key_pos[None, :] <= query_pos[:, None]) & (key_doc[None, :] == query_doc[:, None])


def score_block(query_latent, query_rot, key_lat, key_rot, softmax_scale):
    direct = product('ihr,jr->hij', query_latent, key_lat)
    rotary = product('ihr,jr->hij', query_rot, key_rot)
    return softmax_scale * (direct + rotary)


def stats_update(state, scores, visible, grad_prob):
    row_max, row_sum, row_dot = state
    masked = jnp.where(visible[None], scores, NEGATIVE)
    new_max = jnp.maximum(row_max, jnp.max(masked, axis=2))
    attend = jnp.where(visible[None], jnp.exp(scores - new_max[:, :, None]), 0.0)
    factor = jnp.exp(row_max - new_max)
    return (new_max, row_sum * factor + jnp.sum(attend, axis=2), row_dot * factor + jnp.sum(attend * grad_prob, axis=2))


def grad_update(state, scores, visible, grad_prob, log_total, inner_mean, key_lat, key_rot, query_latent, query_rot, output_grad, key_first, softmax_scale):
    acc_query, acc_rot, acc_out, acc_keys, acc_keyrot = state
    attend = jnp.where(visible[None], jnp.exp(scores - log_total[:, :, None]), 0.0)
    attend_low = attend.astype(jnp.bfloat16)
    grad_score = (attend * (grad_prob - inner_mean[:, :, None])).astype(jnp.bfloat16)
    acc_query = acc_query + product('hij,jr->ihr', grad_score, key_lat)
    acc_rot = acc_rot + product('hij,jr->ihr', grad_score, key_rot)
    acc_out = acc_out + product('hij,jr->ihr', attend_low, key_lat)
    key_part = softmax_scale * product('hij,ihr->jr', grad_score, query_latent) + product('hij,ihr->jr', attend_low, output_grad)
    rot_part = softmax_scale * product('hij,ihr->jr', grad_score, query_rot)
    extent = key_lat.shape[0]
    acc_keys = lax.dynamic_update_slice_in_dim(acc_keys, lax.dynamic_slice_in_dim(acc_keys, key_first, extent, 0) + key_part, key_first, 0)
    acc_keyrot = lax.dynamic_update_slice_in_dim(acc_keyrot, lax.dynamic_slice_in_dim(acc_keyrot, key_first, extent, 0) + rot_part, key_first, 0)
    return (acc_query, acc_rot, acc_out, acc_keys, acc_keyrot)


def one_sequence(query_nope, query_rope, latent, key_rope, grad_output, kv_up, doc_lengths):
    softmax_scale = (HEAD_DIM + ROPE_DIM) ** -0.5
    weights = kv_up.reshape(LATENT, HEAD_COUNT, HEAD_DIM + VALUE_DIM)
    key_weight = weights[:, :, :HEAD_DIM]
    value_weight = weights[:, :, HEAD_DIM:]
    nope_rows = query_nope.reshape(SEQ_LEN, HEAD_COUNT, HEAD_DIM)
    rope_rows = query_rope.reshape(SEQ_LEN, HEAD_COUNT, ROPE_DIM)
    grad_rows = grad_output.reshape(SEQ_LEN, HEAD_COUNT, VALUE_DIM)
    query_latent = product('ihd,rhd->ihr', nope_rows, key_weight).astype(jnp.bfloat16)
    output_grad = product('ihe,rhe->ihr', grad_rows, value_weight).astype(jnp.bfloat16)
    positions = jnp.arange(SEQ_LEN, dtype=jnp.int32)
    query_doc, query_start = doc_bounds(doc_lengths, positions)
    query_block = min(SEQ_LEN, 256)
    key_block = min(SEQ_LEN, 512)
    blocks = SEQ_LEN // query_block

    def per_block(keys_state, inputs):
        block_latent, block_rot, block_grad, block_pos, block_doc, block_start = inputs
        query_last = block_pos[query_block - 1]
        query_floor = block_start[0]

        def skipped(key_first):
            return (key_first > query_last) | (key_first + key_block - 1 < query_floor)

        def stats_loop(index, state):
            key_first = (index * key_block).astype(jnp.int32)
            key_lat = lax.dynamic_slice_in_dim(latent, key_first, key_block, 0)
            key_rot = lax.dynamic_slice_in_dim(key_rope, key_first, key_block, 0)

            def work(inner_state):
                scores = score_block(block_latent, block_rot, key_lat, key_rot, softmax_scale)
                visible = visible_block(block_pos, block_doc, key_first, key_block, doc_lengths)
                grad_prob = product('ihr,jr->hij', block_grad, key_lat)
                return stats_update(inner_state, scores, visible, grad_prob)

            return lax.cond(skipped(key_first), lambda inner_state: inner_state, work, state)

        first_state = (jnp.full((HEAD_COUNT, query_block), NEGATIVE, jnp.float32), jnp.zeros((HEAD_COUNT, query_block), jnp.float32), jnp.zeros((HEAD_COUNT, query_block), jnp.float32))
        row_max, row_sum, row_dot = lax.fori_loop(0, SEQ_LEN // key_block, stats_loop, first_state)
        log_total = row_max + jnp.log(row_sum)
        inner_mean = row_dot / row_sum

        def grad_loop(index, state):
            key_first = (index * key_block).astype(jnp.int32)
            key_lat = lax.dynamic_slice_in_dim(latent, key_first, key_block, 0)
            key_rot = lax.dynamic_slice_in_dim(key_rope, key_first, key_block, 0)

            def work(inner_state):
                scores = score_block(block_latent, block_rot, key_lat, key_rot, softmax_scale)
                visible = visible_block(block_pos, block_doc, key_first, key_block, doc_lengths)
                grad_prob = product('ihr,jr->hij', block_grad, key_lat)
                return grad_update(inner_state, scores, visible, grad_prob, log_total, inner_mean, key_lat, key_rot, block_latent, block_rot, block_grad, key_first, softmax_scale)

            return lax.cond(skipped(key_first), lambda inner_state: inner_state, work, state)

        grad_state = (jnp.zeros((query_block, HEAD_COUNT, LATENT), jnp.float32), jnp.zeros((query_block, HEAD_COUNT, ROPE_DIM), jnp.float32), jnp.zeros((query_block, HEAD_COUNT, LATENT), jnp.float32), keys_state[0], keys_state[1])
        acc_query, acc_rot, acc_out, acc_keys, acc_keyrot = lax.fori_loop(0, SEQ_LEN // key_block, grad_loop, grad_state)
        return (acc_keys, acc_keyrot), (acc_query, acc_rot, acc_out)

    inputs = (query_latent.reshape(blocks, query_block, HEAD_COUNT, LATENT), rope_rows.reshape(blocks, query_block, HEAD_COUNT, ROPE_DIM), output_grad.reshape(blocks, query_block, HEAD_COUNT, LATENT), positions.reshape(blocks, query_block), query_doc.reshape(blocks, query_block), query_start.reshape(blocks, query_block))
    keys_state = (jnp.zeros((SEQ_LEN, LATENT), jnp.float32), jnp.zeros((SEQ_LEN, ROPE_DIM), jnp.float32))
    keys_state, stacked = lax.scan(per_block, keys_state, inputs)
    acc_query = stacked[0].reshape(SEQ_LEN, HEAD_COUNT, LATENT)
    acc_rot = stacked[1].reshape(SEQ_LEN, HEAD_COUNT, ROPE_DIM)
    acc_out = stacked[2].reshape(SEQ_LEN, HEAD_COUNT, LATENT)
    query_latent_grad = (softmax_scale * acc_query).astype(jnp.bfloat16)
    grad_query_rope = (softmax_scale * acc_rot).astype(jnp.bfloat16).reshape(SEQ_LEN, HEAD_COUNT * ROPE_DIM)
    out_latent = acc_out.astype(jnp.bfloat16)
    grad_query_nope = product('ihr,rhd->ihd', query_latent_grad, key_weight).astype(jnp.bfloat16).reshape(SEQ_LEN, HEAD_COUNT * HEAD_DIM)
    weight_term = jnp.concatenate([product('ihr,ihd->rhd', query_latent_grad, nope_rows), product('ihr,ihe->rhe', out_latent, grad_rows)], axis=2).reshape(LATENT, HEAD_COUNT * (HEAD_DIM + VALUE_DIM))
    return (grad_query_nope, grad_query_rope, keys_state[0].astype(jnp.bfloat16), keys_state[1].astype(jnp.bfloat16), weight_term)


def reference(query_nope, query_rope, latent, key_rope, grad_output, kv_up, doc_lengths):
    def run_one(inputs):
        return one_sequence(inputs[0], inputs[1], inputs[2], inputs[3], inputs[4], kv_up, inputs[5])

    results = lax.map(run_one, (query_nope, query_rope, latent, key_rope, grad_output, doc_lengths))
    grad_kv_up = jnp.sum(results[4], axis=0)
    return (results[0], results[1], results[2], results[3], grad_kv_up)
```

```python
import functools
import math

import jax
import jax.numpy as jnp
from jax import lax
from jax.experimental import pallas as pl
from jax.experimental.pallas import tpu as pltpu
from jax.sharding import PartitionSpec as P

HEADS = 16
DIM = 128
ROPE = 64
LATENT = 512
BLOCK = 128
SEQ = 2048
GROUP = 4
SCALE = (DIM + ROPE) ** -0.5
NEGATIVE = -1e30
MESH = pl.DeviceIdType.MESH
VMEM = pltpu.VMEM
F32 = jnp.float32
BF16 = jnp.bfloat16
MIB = 1 << 20


def coords():
    dp, ctx = lax.axis_index("dp"), lax.axis_index("ctx")
    return dp // 8, (dp // 2) % 4, dp % 2, ctx // 4, ctx % 4


def device(zh, y, c, x, z):
    return ((zh * 4 + y) * 2 + c, x * 4 + z)


def remote(src, dst, send, recv, target):
    return pltpu.make_async_remote_copy(
        src_ref=src, dst_ref=dst, send_sem=send, recv_sem=recv, device_id=target, device_id_type=MESH
    )


def greet(targets):
    barrier = pltpu.get_barrier_semaphore()
    for target in targets:
        pl.semaphore_signal(barrier, inc=1, device_id=target, device_id_type=MESH)
    pl.semaphore_wait(barrier, len(targets))


def dot_bt(left, right):
    return lax.dot_general(left, right, (((1,), (1,)), ((), ())), preferred_element_type=F32)


def dot(left, right):
    return jnp.dot(left, right, preferred_element_type=F32)


def gather_kernel(
    nope, rope, gout, lat, krope, lens,
    o_nope, o_gout, o_rope, o_keys, o_lens,
    kblk, q_send, q_recv, kx_send, kx_recv, kz_send, kz_recv, ks_send, ks_recv, l_sem, loc,
):
    zh, y, c, x, z = coords()
    s = x // 2
    sib = device(zh, y, 1 - c, x, z)
    others = [device(zh, y, c, (x + d) % 4, z) for d in (1, 2, 3)]
    others += [device(zh, y, 1 - c, (x + d) % 4, z) for d in (0, 1, 2, 3)]
    others += [device(zh, y, c, x, (z + d) % 4) for d in (1, 2, 3)]
    kblk[:, 0:LATENT] = lat[...]
    pair = krope[...]
    kblk[:, LATENT:LATENT + 2 * ROPE] = jnp.concatenate([pair, pair], axis=1)
    greet(others)

    def rows(at):
        return pl.ds(pl.multiple_of(at * BLOCK, BLOCK), BLOCK)

    home = 4 * x + z

    def key_send(t):
        return remote(kblk, o_keys.at[rows(home)], kx_send.at[t], kx_recv.at[x // 2], device(zh, y, x % 2, 2 * c + t, z))

    def key_local():
        return pltpu.make_async_copy(kblk, o_keys.at[rows(home)], loc.at[0])

    key_self = [(2 * c + t == x) & (x % 2 == c) for t in (0, 1)]
    for t in (0, 1):
        @pl.when(jnp.logical_not(key_self[t]))
        def _():
            key_send(t).start()

        @pl.when(key_self[t])
        def _():
            key_local().start()

    def q_copies(g, target):
        wide = pl.ds(g * GROUP * DIM, GROUP * DIM)
        thin = pl.ds(g * GROUP * ROPE, GROUP * ROPE)
        return [
            remote(nope.at[:, wide], o_nope.at[rows(x)], q_send.at[0, g], q_recv.at[0, x], target),
            remote(gout.at[:, wide], o_gout.at[rows(x)], q_send.at[1, g], q_recv.at[1, x], target),
            remote(rope.at[:, thin], o_rope.at[rows(x)], q_send.at[2, g], q_recv.at[2, x], target),
        ]

    def q_local(g):
        wide = pl.ds(g * GROUP * DIM, GROUP * DIM)
        thin = pl.ds(g * GROUP * ROPE, GROUP * ROPE)
        return [
            pltpu.make_async_copy(nope.at[:, wide], o_nope.at[rows(x)], loc.at[1]),
            pltpu.make_async_copy(gout.at[:, wide], o_gout.at[rows(x)], loc.at[2]),
            pltpu.make_async_copy(rope.at[:, thin], o_rope.at[rows(x)], loc.at[3]),
        ]

    q_self = [(2 * c + g // 2 == x) & (c == g % 2) for g in range(4)]
    for g in range(4):
        @pl.when(jnp.logical_not(q_self[g]))
        def _():
            for copy in q_copies(g, device(zh, y, g % 2, 2 * c + g // 2, z)):
                copy.start()

        @pl.when(q_self[g])
        def _():
            for copy in q_local(g):
                copy.start()

    lens_copy = remote(lens, o_lens, l_sem.at[0], l_sem.at[1], sib)
    lens_copy.start()

    def z_copy(k, d):
        at = rows(4 * (c + 2 * k) + z)
        return remote(o_keys.at[at], o_keys.at[at], kz_send.at[k, d - 1], kz_recv.at[k, d - 1], device(zh, y, c, x, (z + d) % 4))

    def sib_copy(k, d):
        at = rows(4 * (c + 2 * k) + (z + 4 - d) % 4)
        return remote(o_keys.at[at], o_keys.at[at], ks_send.at[k, d], ks_recv.at[k, d], sib)

    for k in (0, 1):
        own = c + 2 * k
        self_here = (own == x) & (s == c)

        @pl.when(jnp.logical_not(self_here))
        def _():
            remote(kblk, o_keys.at[rows(4 * own + z)], kx_send.at[0], kx_recv.at[k], sib).wait_recv()

        @pl.when(self_here)
        def _():
            key_local().wait()

        for d in (1, 2, 3):
            z_copy(k, d).start()
        sib_copy(k, 0).start()

    def z_arrival(k, d):
        at = rows(4 * (c + 2 * k) + (z + 4 - d) % 4)
        return remote(o_keys.at[at], o_keys.at[at], kz_send.at[k, d - 1], kz_recv.at[k, d - 1], device(zh, y, c, x, (z + 4 - d) % 4))

    def sib_arrival(k, d):
        at = rows(4 * (1 - c + 2 * k) + (z + 4 - d) % 4)
        return remote(o_keys.at[at], o_keys.at[at], ks_send.at[k, d], ks_recv.at[k, d], sib)

    for d in (1, 3, 2):
        for k in (0, 1):
            z_arrival(k, d).wait_recv()
            sib_copy(k, d).start()
    for d in (0, 1, 3, 2):
        for k in (0, 1):
            sib_arrival(k, d).wait_recv()

    for xs in range(4):
        self_here = (xs == x) & (s == c)

        @pl.when(jnp.logical_not(self_here))
        def _():
            at = rows(xs)
            remote(nope.at[:, 0:GROUP * DIM], o_nope.at[at], q_send.at[0, 0], q_recv.at[0, xs], sib).wait_recv()
            remote(gout.at[:, 0:GROUP * DIM], o_gout.at[at], q_send.at[1, 0], q_recv.at[1, xs], sib).wait_recv()
            remote(rope.at[:, 0:GROUP * ROPE], o_rope.at[at], q_send.at[2, 0], q_recv.at[2, xs], sib).wait_recv()
    for g in range(4):
        @pl.when(q_self[g])
        def _():
            for copy in q_local(g):
                copy.wait()

        @pl.when(jnp.logical_not(q_self[g]))
        def _():
            for copy in q_copies(g, sib):
                copy.wait_send()
    for t in (0, 1):
        @pl.when(jnp.logical_not(key_self[t]))
        def _():
            key_send(t).wait_send()
    for k in (0, 1):
        for d in (1, 2, 3):
            z_copy(k, d).wait_send()
        for d in (0, 1, 2, 3):
            sib_copy(k, d).wait_send()
    lens_copy.wait()


CHUNK = 256
PAIR = 2 * BLOCK


def fold(values, op):
    return op(values.reshape(values.shape[0] // 8, 8, values.shape[1]), axis=0)


def attend_kernel(
    lens, qn, go, qr, keys, w,
    o_qn, o_qr, o_keys, o_w,
    kx, vx, ktx, qx, st, dpt, dkv, dkr, dqt, latt,
):
    ctx = lax.axis_index("ctx")
    z = ctx % 4
    chunk = 512
    lane = lax.broadcasted_iota(jnp.int32, (1, 2 * ROPE), 1)

    for h in range(GROUP):
        qx[:, h * 256:h * 256 + DIM] = qn[:, h * DIM:(h + 1) * DIM]
        half = qr[:, (h // 2) * 128:(h // 2) * 128 + 128]
        keep = (lane < ROPE) if h % 2 == 0 else (lane >= ROPE)
        qx[:, h * 256 + DIM:(h + 1) * 256] = jnp.where(keep, half, jnp.zeros_like(half))
    wt = [w[:, h * 256:h * 256 + DIM].T for h in range(GROUP)]

    def project(i, carry):
        at = pl.ds(pl.multiple_of(i * chunk, chunk), chunk)
        rows = keys[at, 0:LATENT]
        rot = keys[at, LATENT:LATENT + 128]
        rot_t = rot.T
        for h in range(GROUP):
            both = dot(rows, w[:, h * 256:(h + 1) * 256]).astype(BF16)
            kx[at, h * 256:h * 256 + DIM] = both[:, 0:DIM]
            kx[at, h * 256 + DIM:(h + 1) * 256] = rot
            vx[at, h * DIM:(h + 1) * DIM] = both[:, DIM:256]
            ktx[h, 0:DIM, at] = dot_bt(wt[h], rows).astype(BF16)
            ktx[h, DIM:256, at] = rot_t
        latt[:, at] = rows.T
        dkv[at, :] = jnp.zeros((chunk, GROUP * 256), BF16)
        dkr[at, :] = jnp.zeros((chunk, 128), F32)
        return carry

    lax.fori_loop(0, SEQ // chunk, project, 0)

    row_lane = lax.broadcasted_iota(jnp.int32, (1, PAIR), 1)
    for t in (1, 0):
        at_rows = slice(t * PAIR, (t + 1) * PAIR)
        pos = (4 * (2 * t + row_lane // BLOCK) + z) * BLOCK + row_lane % BLOCK
        first_pos = (8 * t + z) * BLOCK
        start = jnp.zeros_like(pos)
        floor = jnp.int32(0)
        end = jnp.int32(0)
        for d in range(8):
            end = end + lens[d]
            start = jnp.maximum(start, jnp.where(end <= pos, end, 0))
            floor = jnp.maximum(floor, jnp.where(end <= first_pos, end, 0))
        low = floor // CHUNK
        high = (8 * t + 6 + z) // 2

        def scores(i, carry):
            at = pl.ds(pl.multiple_of(i * CHUNK, CHUNK), CHUNK)
            key = lax.broadcasted_iota(jnp.int32, (CHUNK, PAIR), 0) + i * CHUNK
            seen = (key <= pos) & (key >= start)
            out = []
            for h in range(GROUP):
                s = dot_bt(kx[at, h * 256:(h + 1) * 256], qx[at_rows, h * 256:(h + 1) * 256])
                s = jnp.where(seen, s * (SCALE * math.log2(math.e)), NEGATIVE)
                st[h, at, :] = s
                out.append(jnp.maximum(carry[h], fold(s, jnp.max)))
            return tuple(out)

        tops = lax.fori_loop(low, high, scores, tuple(jnp.full((8, PAIR), NEGATIVE, F32) for h in range(GROUP)))
        top = [jnp.max(tops[h], axis=0, keepdims=True) for h in range(GROUP)]

        def sums(i, carry):
            at = pl.ds(pl.multiple_of(i * CHUNK, CHUNK), CHUNK)
            out = []
            for h in range(GROUP):
                p = jnp.exp2(st[h, at, :] - top[h])
                d = dot_bt(vx[at, h * DIM:(h + 1) * DIM], go[at_rows, h * DIM:(h + 1) * DIM])
                st[h, at, :] = p
                dpt[h, at, :] = d
                out.append(carry[2 * h] + fold(p, jnp.sum))
                out.append(carry[2 * h + 1] + fold(p * d, jnp.sum))
            return tuple(out)

        totals = lax.fori_loop(low, high, sums, tuple(jnp.zeros((8, PAIR), F32) for h in range(2 * GROUP)))
        inv = [1.0 / jnp.sum(totals[2 * h], axis=0, keepdims=True) for h in range(GROUP)]
        inner = [jnp.sum(totals[2 * h + 1], axis=0, keepdims=True) * inv[h] for h in range(GROUP)]
        for h in range(GROUP):
            dqt[h] = jnp.zeros((256, PAIR), F32)

        def grads(i, carry):
            at = pl.ds(pl.multiple_of(i * CHUNK, CHUNK), CHUNK)
            rot = dkr[at, :]
            for h in range(GROUP):
                p = st[h, at, :] * inv[h]
                ds = ((p * SCALE) * (dpt[h, at, :] - inner[h])).astype(BF16)
                low_p = p.astype(BF16)
                dk = dot(ds, qx[at_rows, h * 256:(h + 1) * 256])
                dv = dot(low_p, go[at_rows, h * DIM:(h + 1) * DIM])
                dqt[h] += dot(ktx[h, :, at], ds)
                rot = rot + dk[:, DIM:256]
                both = jnp.concatenate([dk[:, 0:DIM], dv], axis=1)
                if t == 0:
                    both = both + dkv[at, h * 256:(h + 1) * 256].astype(F32)
                dkv[at, h * 256:(h + 1) * 256] = both.astype(BF16)
            dkr[at, :] = rot
            return carry

        lax.fori_loop(low, high, grads, 0)
        rots = []
        for h in range(GROUP):
            dq = dqt[h].T
            o_qn[at_rows, h * DIM:(h + 1) * DIM] = dq[:, 0:DIM].astype(BF16)
            rots.append(dq[:, DIM:256])
        for p in (0, 1):
            o_qr[at_rows, p * 128:(p + 1) * 128] = jnp.where(lane < ROPE, rots[2 * p], rots[2 * p + 1]).astype(BF16)

    def back(i, carry):
        at = pl.ds(pl.multiple_of(i * chunk, chunk), chunk)
        o_keys[at, 0:LATENT] = dot_bt(dkv[at, :], w[...]).astype(BF16)
        rot = dkr[at, :]
        o_keys[at, LATENT:LATENT + 128] = (rot + pltpu.roll(rot, ROPE, 1)).astype(BF16)
        return carry

    lax.fori_loop(0, SEQ // chunk, back, 0)
    for n in range(GROUP):
        o_w[:, n * 256:(n + 1) * 256] = dot(latt[...], dkv[:, n * 256:(n + 1) * 256]).astype(BF16)


def reduce_kernel(
    dqn, dqr, dkp, wp,
    o_qn, o_qr, o_lat, o_rot, o_w,
    sin, acc, zin, fin, hin, yin, ys, cin, cs, hi_in, fs, ag,
    q_send, q_recv, s_send, s_recv, z_send, z_recv, h_send, h_recv, y_send, y_recv, c_send, c_recv, hi_sem, a_send, a_recv, loc,
):
    zh, y, c, x, z = coords()
    s = x // 2
    g = 2 * (x % 2) + c
    ctx = 4 * x + z
    sib = device(zh, y, 1 - c, x, z)
    others = [device(zh, y, c, (x + dx) % 4, (z + dz) % 4) for dx in range(4) for dz in range(4) if dx or dz]
    others += [device(zh, y, 1 - c, (x + d) % 4, z) for d in range(4)]
    others += [device(zh, (y + d) % 4, cc, x, z) for d in (1, 2, 3) for cc in (0, 1)]
    others += [device(1 - zh, y, c, x, z)]
    greet(others)

    def rows(at, size=BLOCK):
        return pl.ds(pl.multiple_of(at * BLOCK, BLOCK), size)

    def s_copy(k):
        return remote(dkp.at[rows(4 * (1 - c + 2 * k), 512)], sin.at[k], s_send.at[k], s_recv.at[k], sib)

    for k in (0, 1):
        s_copy(k).start()

    def y_copy(d):
        peer = (y + d) % 4
        return remote(wp.at[:, pl.ds(pl.multiple_of(peer * 256, 256), 256)], yin.at[d - 1], y_send.at[d - 1], y_recv.at[d - 1], device(zh, peer, c, x, z))

    for d in (1, 3, 2):
        y_copy(d).start()

    def q_copies(xs):
        target = device(zh, y, s, xs, z)
        at = rows(xs)
        wide = pl.ds(pl.multiple_of(g * GROUP * DIM, GROUP * DIM), GROUP * DIM)
        thin = pl.ds(pl.multiple_of(g * GROUP * ROPE, GROUP * ROPE), GROUP * ROPE)
        return [
            remote(dqn.at[at], o_qn.at[:, wide], q_send.at[0, xs], q_recv.at[0, g], target),
            remote(dqr.at[at], o_qr.at[:, thin], q_send.at[1, xs], q_recv.at[1, g], target),
        ]

    def q_local():
        at = rows(x)
        wide = pl.ds(pl.multiple_of(g * GROUP * DIM, GROUP * DIM), GROUP * DIM)
        thin = pl.ds(pl.multiple_of(g * GROUP * ROPE, GROUP * ROPE), GROUP * ROPE)
        return [
            pltpu.make_async_copy(dqn.at[at], o_qn.at[:, wide], loc.at[0]),
            pltpu.make_async_copy(dqr.at[at], o_qr.at[:, thin], loc.at[1]),
        ]

    q_self = [(xs == x) & (s == c) for xs in range(4)]
    for xs in range(4):
        @pl.when(jnp.logical_not(q_self[xs]))
        def _():
            for copy in q_copies(xs):
                copy.start()

        @pl.when(q_self[xs])
        def _():
            for copy in q_local():
                copy.start()

    def z_copy(k, d):
        peer = (z + d) % 4
        return remote(acc.at[k, rows(peer)], zin.at[d - 1, k], z_send.at[k, d - 1], z_recv.at[k, d - 1], device(zh, y, c, x, peer))

    for k in (0, 1):
        s_copy(k).wait_recv()
        acc[k] = (dkp[rows(4 * (c + 2 * k), 512), :].astype(F32) + sin[k].astype(F32)).astype(BF16)
        for d in (2, 1, 3):
            z_copy(k, d).start()

    for d in (1, 3, 2):
        y_copy(d).wait_recv()
    mine = wp[:, pl.ds(pl.multiple_of(y * 256, 256), 256)].astype(F32)
    ys[...] = (mine + yin[0].astype(F32) + yin[1].astype(F32) + yin[2].astype(F32)).astype(BF16)

    def c_copy(dx, dz):
        px, pz = (x + dx) % 4, (z + dz) % 4
        src = ys.at[pl.ds(pl.multiple_of((4 * px + pz) * 32, 32), 32)]
        return remote(src, cin.at[dx, dz], c_send.at[dx, dz], c_recv.at[dx, dz], device(zh, y, c, px, pz))

    pairs = [(dx, dz) for dz in (2, 1, 3, 0) for dx in (2, 1, 3, 0) if dx or dz]
    for dx, dz in pairs:
        c_copy(dx, dz).start()

    def h_copy(k):
        return remote(fin.at[k], hin.at[x % 2], h_send.at[k], h_recv.at[x % 2], device(zh, y, s, c + 2 * k, z))

    def h_local(k):
        return pltpu.make_async_copy(fin.at[k], hin.at[x % 2], loc.at[2])

    h_self = [(c + 2 * k == x) & (s == c) for k in (0, 1)]
    for k in (0, 1):
        for d in (1, 3, 2):
            z_copy(k, d).wait_recv()
        total = acc[k, rows(z), :].astype(F32)
        for d in (1, 2, 3):
            total = total + zin[d - 1, k].astype(F32)
        fin[k] = total.astype(BF16)

        @pl.when(jnp.logical_not(h_self[k]))
        def _():
            h_copy(k).start()

        @pl.when(h_self[k])
        def _():
            h_local(k).start()

    for dx, dz in pairs:
        c_copy(dx, dz).wait_recv()
    own = ys[pl.ds(pl.multiple_of(ctx * 32, 32), 32), :].astype(F32)
    even = own
    for dz in (1, 2, 3):
        even = even + cin[0, dz].astype(F32)
    for dz in range(4):
        even = even + cin[2, dz].astype(F32)
    odd = jnp.zeros_like(own)
    for dx in (1, 3):
        for dz in range(4):
            odd = odd + cin[dx, dz].astype(F32)
    flip = x % 2 == 1
    cs[:, 0:256] = jnp.where(flip, odd, even).astype(BF16)
    cs[:, 256:512] = jnp.where(flip, even, odd).astype(BF16)
    hi_copy = remote(cs, hi_in, hi_sem.at[0], hi_sem.at[1], device(1 - zh, y, c, x, z))
    hi_copy.start()

    for t in (0, 1):
        self_here = (2 * c + t == x) & (x % 2 == c)

        @pl.when(jnp.logical_not(self_here))
        def _():
            remote(fin.at[0], hin.at[t], h_send.at[0], h_recv.at[t], sib).wait_recv()
    for k in (0, 1):
        @pl.when(h_self[k])
        def _():
            h_local(k).wait()
    final = hin[0].astype(F32) + hin[1].astype(F32)
    o_lat[...] = final[:, 0:LATENT].astype(BF16)
    o_rot[...] = final[:, LATENT:LATENT + ROPE].astype(BF16)

    hi_copy.wait_recv()
    fs[...] = (cs[...].astype(F32) + hi_in[...].astype(F32)).astype(BF16)

    def a_copy(dy, dc):
        peer = device(zh, (y + dy) % 4, (c + dc) % 2, x, z)
        return remote(fs, ag.at[dy, dc], a_send.at[dy, dc], a_recv.at[dy, dc], peer)

    members = [(dy, dc) for dy in (2, 1, 3, 0) for dc in (0, 1) if dy or dc]
    for dy, dc in members:
        a_copy(dy, dc).start()

    def place(values, from_y, from_c):
        wide = values.astype(F32)
        for p in (0, 1):
            at = pl.multiple_of((2 * p + from_c) * 1024 + from_y * 256, 256)
            o_w[:, pl.ds(at, 256)] = wide[:, p * 256:(p + 1) * 256]

    place(fs[...], y, c)
    for dy, dc in members:
        a_copy(dy, dc).wait_recv()
        place(ag[dy, dc], (y + 4 - dy) % 4, (c + dc) % 2)

    for gs in range(4):
        self_here = (g == gs) & (s == c)

        @pl.when(jnp.logical_not(self_here))
        def _():
            remote(dqn.at[0:BLOCK], o_qn.at[:, gs * GROUP * DIM:(gs + 1) * GROUP * DIM], q_send.at[0, 0], q_recv.at[0, gs], sib).wait_recv()
            remote(dqr.at[0:BLOCK], o_qr.at[:, gs * GROUP * ROPE:(gs + 1) * GROUP * ROPE], q_send.at[1, 0], q_recv.at[1, gs], sib).wait_recv()
    for xs in range(4):
        @pl.when(jnp.logical_not(q_self[xs]))
        def _():
            for copy in q_copies(xs):
                copy.wait_send()

        @pl.when(q_self[xs])
        def _():
            for copy in q_local():
                copy.wait()
    for k in (0, 1):
        s_copy(k).wait_send()
        for d in (1, 2, 3):
            z_copy(k, d).wait_send()

        @pl.when(jnp.logical_not(h_self[k]))
        def _():
            h_copy(k).wait_send()
    for d in (1, 2, 3):
        y_copy(d).wait_send()
    for dx, dz in pairs:
        c_copy(dx, dz).wait_send()
    hi_copy.wait_send()
    for dy, dc in members:
        a_copy(dy, dc).wait_send()


def vmem():
    return pl.BlockSpec(memory_space=pltpu.VMEM)


def shape(dims, kind=BF16):
    return jax.ShapeDtypeStruct(dims, kind)


def dma(*dims):
    return pltpu.SemaphoreType.DMA(dims)


def gather(nope, rope, gout, lat, krope, lens):
    return pl.pallas_call(
        gather_kernel,
        name="gather_rows",
        out_shape=(
            shape((512, GROUP * DIM)),
            shape((512, GROUP * DIM)),
            shape((512, GROUP * ROPE)),
            shape((SEQ, LATENT + 128)),
            shape((8, 128), jnp.int32),
        ),
        in_specs=[vmem()] * 6,
        out_specs=(vmem(),) * 5,
        scratch_shapes=[
            VMEM((BLOCK, LATENT + 128), BF16),
            dma(3, 4), dma(3, 4), dma(2), dma(2), dma(2, 3), dma(2, 3), dma(2, 4), dma(2, 4), dma(2), dma(4),
        ],
        compiler_params=pltpu.CompilerParams(collective_id=0, has_side_effects=True, vmem_limit_bytes=24 * MIB),
    )(nope, rope, gout, lat, krope, lens)


def attend(lens, qn, go, qr, keys, w):
    return pl.pallas_call(
        attend_kernel,
        name="attend_rows",
        out_shape=(
            shape((512, GROUP * DIM)),
            shape((512, GROUP * ROPE)),
            shape((SEQ, LATENT + 128)),
            shape((LATENT, GROUP * 256)),
        ),
        in_specs=[pl.BlockSpec(memory_space=pltpu.SMEM)] + [vmem()] * 5,
        out_specs=(vmem(),) * 4,
        scratch_shapes=[
            VMEM((SEQ, GROUP * 256), BF16),
            VMEM((SEQ, GROUP * DIM), BF16),
            VMEM((GROUP, 256, SEQ), BF16),
            VMEM((512, GROUP * 256), BF16),
            VMEM((GROUP, SEQ, PAIR), F32),
            VMEM((GROUP, SEQ, PAIR), F32),
            VMEM((SEQ, GROUP * 256), BF16),
            VMEM((SEQ, 128), F32),
            VMEM((GROUP, 256, PAIR), F32),
            VMEM((LATENT, SEQ), BF16),
        ],
        compiler_params=pltpu.CompilerParams(vmem_limit_bytes=56 * MIB),
    )(lens, qn, go, qr, keys, w)


def reduce(dqn, dqr, dkp, wp):
    return pl.pallas_call(
        reduce_kernel,
        name="reduce_rows",
        out_shape=(
            shape((BLOCK, HEADS * DIM)),
            shape((BLOCK, HEADS * ROPE)),
            shape((BLOCK, LATENT)),
            shape((BLOCK, ROPE)),
            shape((32, HEADS * 256), F32),
        ),
        in_specs=[vmem()] * 4,
        out_specs=(vmem(),) * 5,
        scratch_shapes=[
            VMEM((2, 512, 640), BF16),
            VMEM((2, 512, 640), BF16),
            VMEM((3, 2, BLOCK, 640), BF16),
            VMEM((2, BLOCK, 640), BF16),
            VMEM((2, BLOCK, 640), BF16),
            VMEM((3, 512, 256), BF16),
            VMEM((512, 256), BF16),
            VMEM((4, 4, 32, 256), BF16),
            VMEM((32, 512), BF16),
            VMEM((32, 512), BF16),
            VMEM((32, 512), BF16),
            VMEM((4, 2, 32, 512), BF16),
            dma(2, 4), dma(2, 4), dma(2), dma(2), dma(2, 3), dma(2, 3), dma(2), dma(2), dma(3), dma(3),
            dma(4, 4), dma(4, 4), dma(2), dma(4, 2), dma(4, 2), dma(3),
        ],
        compiler_params=pltpu.CompilerParams(collective_id=1, has_side_effects=True, vmem_limit_bytes=40 * MIB),
    )(dqn, dqr, dkp, wp)


def body(query_nope, query_rope, latent, key_rope, grad_output, kv_up, doc_lengths):
    dp, ctx = lax.axis_index("dp"), lax.axis_index("ctx")
    c, x = dp % 2, ctx // 4
    own = jnp.pad(doc_lengths, ((0, 7), (0, 120)))
    qn, go, qr, keys, other = gather(query_nope[0], query_rope[0], grad_output[0], latent[0], key_rope[0], own)
    lens = jnp.where(x // 2 == c, own[0, :8], other[0, :8])
    g = 2 * (x % 2) + c
    w = lax.dynamic_slice_in_dim(kv_up, g * GROUP * 256, GROUP * 256, 1)
    dqn, dqr, dkp, wp = attend(lens, qn, go, qr, keys, w)
    gqn, gqr, glat, grot, gw = reduce(dqn, dqr, dkp, wp)
    return gqn[None], gqr[None], glat[None], grot[None], gw


def solution(mesh):
    rows = P("dp", "ctx", None)
    return jax.shard_map(
        body,
        mesh=mesh,
        in_specs=(rows, rows, rows, rows, rows, P(), P("dp", None)),
        out_specs=(rows, rows, rows, rows, P("ctx", None)),
        check_vma=False,
    )
```

```python
import functools
import math

import jax
import jax.numpy as jnp
from jax import lax
from jax.experimental import pallas as pl
from jax.experimental.pallas import tpu as pltpu
from jax.sharding import PartitionSpec as P

HEADS = 16
DIM = 128
ROPE = 64
LATENT = 512
BLOCK = 128
SEQ = 2048
GROUP = 4
SCALE = (DIM + ROPE) ** -0.5
NEGATIVE = -1e30
MESH = pl.DeviceIdType.MESH
VMEM = pltpu.VMEM
F32 = jnp.float32
BF16 = jnp.bfloat16
MIB = 1 << 20


def coords():
    dp, ctx = lax.axis_index("dp"), lax.axis_index("ctx")
    return dp // 8, (dp // 2) % 4, dp % 2, ctx // 4, ctx % 4


def device(zh, y, c, x, z):
    return ((zh * 4 + y) * 2 + c, x * 4 + z)


def remote(src, dst, send, recv, target):
    return pltpu.make_async_remote_copy(
        src_ref=src, dst_ref=dst, send_sem=send, recv_sem=recv, device_id=target, device_id_type=MESH
    )


def greet(targets):
    barrier = pltpu.get_barrier_semaphore()
    for target in targets:
        pl.semaphore_signal(barrier, inc=1, device_id=target, device_id_type=MESH)
    pl.semaphore_wait(barrier, len(targets))


def dot_bt(left, right):
    return lax.dot_general(left, right, (((1,), (1,)), ((), ())), preferred_element_type=F32)


def dot(left, right):
    return jnp.dot(left, right, preferred_element_type=F32)


PAIR = 2 * BLOCK
WIDE = 4 * BLOCK
HALF = BLOCK // 2
KEYS = LATENT + 2 * ROPE


def fold(values, op):
    return op(values.reshape(values.shape[0] // 8, 8, values.shape[1]), axis=0)


def across(a, p):
    return (a % 2 + p % 2) % 2 + 2 * ((a // 2 + p // 2) % 2)


def kernel(
    nope, rope, gout, lat, krope, lens, kv_up,
    o_qn, o_qr, o_lat, o_rot, o_w,
    kblk, w, qn, go, qr, own_lens, other_lens, keys, zstage,
    kx, vx, ktx, qx, st0, st1, stats, dkv, dkr, dqt, latt, dqn, dqr, wp,
    dkp, sin, acc, zin, fin, hin, xin, xsum, zfin, yin, ys, cin, cs, hi_in, fs, ag,
    q_send, q_recv, kx_send, kx_recv, kz_send, kz_recv, ks_send, ks_recv, l_sem, loc,
    zs_send, zs_recv, kf_send, kf_recv, kf_loc,
    d_send, d_recv, s_send, s_recv, z_send, z_recv, h_send, h_recv, x_send, x_recv, x_loc, zf_send, zf_recv,
    y_send, y_recv, c_send, c_recv, hi_sem, a_send, a_recv,
):
    zh, y, c, x, z = coords()
    s = x // 2
    group = 2 * (x % 2) + c
    sib = device(zh, y, 1 - c, x, z)
    others = [device(zh, y, c, (x + dx) % 4, (z + dz) % 4) for dx in range(4) for dz in range(4) if dx or dz]
    others += [device(zh, y, 1 - c, (x + d) % 4, z) for d in range(4)]
    others += [device(zh, (y + d) % 4, cc, x, z) for d in (1, 2, 3) for cc in (0, 1)]
    others += [device(1 - zh, y, c, x, z)]
    lane = lax.broadcasted_iota(jnp.int32, (1, 2 * ROPE), 1)

    def rows(at, size=BLOCK):
        return pl.ds(pl.multiple_of(at * BLOCK, BLOCK), size)

    def wide_rows(p):
        return pl.ds(pl.multiple_of(p * WIDE, WIDE), WIDE)

    w_copy = pltpu.make_async_copy(kv_up.at[:, pl.ds(pl.multiple_of(group * 1024, 1024), 1024)], w, loc.at[4])
    w_copy.start()
    kblk[:, 0:LATENT] = lat[...]
    pair = krope[...].T
    own_lens[...] = jnp.zeros(own_lens.shape, jnp.int32)
    own_lens[0:1, 0:8] = lens[...]
    kblk[:, LATENT:KEYS] = jnp.concatenate([pair, pair], axis=1)
    greet(others)

    def key_send(t):
        return remote(kblk, keys.at[rows(x)], kx_send.at[t], kx_recv.at[x // 2], device(zh, y, x % 2, 2 * c + t, z))

    def key_local():
        return pltpu.make_async_copy(kblk, keys.at[rows(x)], loc.at[0])

    key_self = [(2 * c + t == x) & (x % 2 == c) for t in (0, 1)]
    for t in (0, 1):
        @pl.when(jnp.logical_not(key_self[t]))
        def _():
            key_send(t).start()

        @pl.when(key_self[t])
        def _():
            key_local().start()

    def zs_copy(p):
        return remote(
            kblk.at[HALF:BLOCK], zstage.at[p - 1], zs_send.at[p - 1], zs_recv.at[p - 1], device(zh, y, c, x, across(z, p))
        )

    for p in (1, 2, 3):
        zs_copy(p).start()

    def q_copies(g, target):
        wide = pl.ds(g * GROUP * DIM, GROUP * DIM)
        thin = pl.ds(g * GROUP * ROPE, GROUP * ROPE)
        return [
            remote(nope.at[:, wide], qn.at[rows(x)], q_send.at[0, g], q_recv.at[0, x], target),
            remote(rope.at[:, thin], qr.at[rows(x)], q_send.at[2, g], q_recv.at[2, x], target),
            remote(gout.at[:, wide], go.at[rows(x)], q_send.at[1, g], q_recv.at[1, x], target),
        ]

    def q_local(g):
        wide = pl.ds(g * GROUP * DIM, GROUP * DIM)
        thin = pl.ds(g * GROUP * ROPE, GROUP * ROPE)
        return [
            pltpu.make_async_copy(nope.at[:, wide], qn.at[rows(x)], loc.at[1]),
            pltpu.make_async_copy(gout.at[:, wide], go.at[rows(x)], loc.at[2]),
            pltpu.make_async_copy(rope.at[:, thin], qr.at[rows(x)], loc.at[3]),
        ]

    q_self = [(2 * c + g // 2 == x) & (c == g % 2) for g in range(4)]
    for g in range(4):
        @pl.when(jnp.logical_not(q_self[g]))
        def _():
            for copy in q_copies(g, device(zh, y, g % 2, 2 * c + g // 2, z)):
                copy.start()

        @pl.when(q_self[g])
        def _():
            for copy in q_local(g):
                copy.start()

    lens_copy = remote(own_lens, other_lens, l_sem.at[0], l_sem.at[1], sib)
    lens_copy.start()

    def key_rows(p, k, core):
        return rows(4 * p + core + 2 * k)

    def half_rows(p, k, core, half):
        return pl.ds(pl.multiple_of((4 * p + core + 2 * k) * BLOCK + half * HALF, HALF), HALF)

    def z_key(k, p):
        return remote(
            keys.at[half_rows(0, k, c, 0)], keys.at[half_rows(p, k, c, 0)],
            kz_send.at[k, p - 1], kz_recv.at[k, p - 1], device(zh, y, c, x, across(z, p)),
        )

    def kf_copy(t, p):
        return remote(
            zstage.at[p - 1], keys.at[half_rows(p, x // 2, x % 2, 1)],
            kf_send.at[t, p - 1], kf_recv.at[x // 2, p - 1], device(zh, y, x % 2, 2 * c + t, z),
        )

    def kf_local(p):
        return pltpu.make_async_copy(zstage.at[p - 1], keys.at[half_rows(p, x // 2, x % 2, 1)], kf_loc.at[p - 1])

    def sib_key(k, p, core):
        at = key_rows(p, k, core)
        return remote(keys.at[at], keys.at[at], ks_send.at[k, p], ks_recv.at[k, p], sib)

    for k in (0, 1):
        own = c + 2 * k
        self_here = (own == x) & (s == c)

        @pl.when(jnp.logical_not(self_here))
        def _():
            remote(kblk, keys.at[rows(own)], kx_send.at[0], kx_recv.at[k], sib).wait_recv()

        @pl.when(self_here)
        def _():
            key_local().wait()

        for p in (1, 2, 3):
            z_key(k, p).start()
        sib_key(k, 0, c).start()

    def take(p):
        for k in (0, 1):
            sib_key(k, p, 1 - c).wait_recv()

    def pass_on(p):
        for k in (0, 1):
            z_key(k, p).wait_recv()
            self_here = (c + 2 * k == x) & (s == c)

            @pl.when(jnp.logical_not(self_here))
            def _():
                remote(zstage.at[p - 1], keys.at[half_rows(p, k, c, 1)], kf_send.at[0, p - 1], kf_recv.at[k, p - 1], sib).wait_recv()

            @pl.when(self_here)
            def _():
                kf_local(p).wait()

            sib_key(k, p, c).start()

    w_copy.wait()
    wt = [w[:, h * 256:h * 256 + DIM].T for h in range(GROUP)]

    def project(p):
        at = wide_rows(p)
        own = keys[at, 0:LATENT]
        rot = keys[at, LATENT:KEYS]
        rot_t = rot.T
        for h in range(GROUP):
            both = dot(own, w[:, h * 256:(h + 1) * 256]).astype(BF16)
            kx[at, h * 256:h * 256 + DIM] = both[:, 0:DIM]
            kx[at, h * 256 + DIM:(h + 1) * 256] = rot
            vx[at, h * DIM:(h + 1) * DIM] = both[:, DIM:256]
            ktx[h, 0:DIM, at] = dot_bt(wt[h], own).astype(BF16)
            ktx[h, DIM:256, at] = rot_t
        latt[:, at] = own.T

    take(0)
    project(0)
    for p in (1, 2, 3):
        zs_copy(p).wait_recv()
        for t in (0, 1):
            @pl.when(jnp.logical_not(key_self[t]))
            def _():
                kf_copy(t, p).start()

            @pl.when(key_self[t])
            def _():
                kf_local(p).start()

    lens_copy.wait_recv()
    sizes = jnp.where(s == c, own_lens[0:1, :], other_lens[0:1, :])
    row_lane = lax.broadcasted_iota(jnp.int32, (1, PAIR), 1)
    positions, starts = [], []
    for t in (0, 1):
        pos = (4 * (2 * t + row_lane // BLOCK) + z) * BLOCK + row_lane % BLOCK
        start = jnp.zeros_like(pos)
        end = jnp.zeros_like(sizes[:, 0:1])
        for d in range(8):
            end = end + sizes[:, d:d + 1]
            start = jnp.maximum(start, jnp.where(end <= pos, end, 0))
        positions.append(pos)
        starts.append(start)
    stats[...] = jnp.zeros(stats.shape, F32)
    for h in range(GROUP):
        for t in (0, 1):
            stats[h, t, 0] = jnp.full((8, PAIR), NEGATIVE, F32)
    dqt[...] = jnp.zeros(dqt.shape, F32)

    for xs in range(4):
        self_here = (xs == x) & (s == c)

        @pl.when(jnp.logical_not(self_here))
        def _():
            at = rows(xs)
            remote(nope.at[:, 0:GROUP * DIM], qn.at[at], q_send.at[0, 0], q_recv.at[0, xs], sib).wait_recv()
            remote(rope.at[:, 0:GROUP * ROPE], qr.at[at], q_send.at[2, 0], q_recv.at[2, xs], sib).wait_recv()
            remote(gout.at[:, 0:GROUP * DIM], go.at[at], q_send.at[1, 0], q_recv.at[1, xs], sib).wait_recv()
    for g in range(4):
        @pl.when(q_self[g])
        def _():
            for copy in q_local(g):
                copy.wait()
    for h in range(GROUP):
        qx[:, h * 256:h * 256 + DIM] = qn[:, h * DIM:(h + 1) * DIM]
        half = qr[:, (h // 2) * 128:(h // 2) * 128 + 128]
        keep = (lane < ROPE) if h % 2 == 0 else (lane >= ROPE)
        qx[:, h * 256 + DIM:(h + 1) * 256] = jnp.where(keep, half, jnp.zeros_like(half))

    pairs = [slice(0, PAIR), slice(PAIR, WIDE)]
    spans = [PAIR, WIDE]
    scores = [st0, st1]

    def span(p, t):
        return pl.ds(pl.multiple_of(p * spans[t], spans[t]), spans[t])

    def key_span(p, t):
        return pl.ds(pl.multiple_of(p * WIDE, WIDE), spans[t])

    def look(p):
        base = lax.broadcasted_iota(jnp.int32, (WIDE, 1), 0)
        key = base + (base // BLOCK) * (3 * BLOCK) + across(z, p) * BLOCK
        for t in (0, 1):
            part = key[0:spans[t]]
            seen = (part <= positions[t]) & (part >= starts[t])
            for h in range(GROUP):
                at = key_span(p, t)
                v = dot_bt(kx[at, h * 256:(h + 1) * 256], qx[pairs[t], h * 256:(h + 1) * 256])
                d = dot_bt(vx[at, h * DIM:(h + 1) * DIM], go[pairs[t], h * DIM:(h + 1) * DIM])
                v = jnp.where(seen, v * (SCALE * math.log2(math.e)), NEGATIVE)
                scores[t][h, span(p, t), :] = v
                old = stats[h, t, 0]
                top = jnp.maximum(old, fold(v, jnp.max))
                e = jnp.exp2(v.reshape(spans[t] // 8, 8, PAIR) - top[None])
                factor = jnp.exp2(old - top)
                stats[h, t, 0] = top
                stats[h, t, 1] = stats[h, t, 1] * factor + jnp.sum(e, axis=0)
                stats[h, t, 2] = stats[h, t, 2] * factor + jnp.sum(e * d.reshape(spans[t] // 8, 8, PAIR), axis=0)

    look(0)

    def arrive(p, carry):
        pass_on(p)
        take(p)
        project(p)
        look(p)
        return carry

    lax.fori_loop(1, 4, arrive, 0)

    logs, inners = [], []
    for h in range(GROUP):
        for t in (0, 1):
            top8 = stats[h, t, 0]
            top = jnp.max(top8, axis=0, keepdims=True)
            factor = jnp.exp2(top8 - top)
            total = jnp.sum(stats[h, t, 1] * factor, axis=0, keepdims=True)
            inners.append(jnp.sum(stats[h, t, 2] * factor, axis=0, keepdims=True) / total)
            logs.append(top + jnp.log2(total))

    def grads(p):
        at = wide_rows(p)
        low = pl.ds(pl.multiple_of(p * WIDE, WIDE), PAIR)
        high = pl.ds(pl.multiple_of(p * WIDE + PAIR, PAIR), PAIR)
        rot_low = jnp.zeros((PAIR, 2 * ROPE), F32)
        rot_high = jnp.zeros((PAIR, 2 * ROPE), F32)
        for h in range(GROUP):
            probs, diffs = [], []
            for t in (0, 1):
                e = jnp.exp2(scores[t][h, span(p, t), :] - logs[2 * h + t])
                d = dot_bt(vx[key_span(p, t), h * DIM:(h + 1) * DIM], go[pairs[t], h * DIM:(h + 1) * DIM])
                diff = (e * (d - inners[2 * h + t])).astype(BF16)
                dqt[h, t] += dot(ktx[h, :, key_span(p, t)], diff)
                probs.append(e.astype(BF16))
                diffs.append(diff)
            q_at, g_at = slice(h * 256, (h + 1) * 256), slice(h * DIM, (h + 1) * DIM)
            dk = SCALE * dot(jnp.concatenate([diffs[0], diffs[1][0:PAIR]], axis=1), qx[:, q_at])
            dv = dot(jnp.concatenate([probs[0], probs[1][0:PAIR]], axis=1), go[:, g_at])
            dkv[low, h * 256:h * 256 + DIM] = dk[:, 0:DIM].astype(BF16)
            dkv[low, h * 256 + DIM:(h + 1) * 256] = dv.astype(BF16)
            rot_low = rot_low + dk[:, DIM:256]
            dk = SCALE * dot(diffs[1][PAIR:WIDE], qx[pairs[1], q_at])
            dv = dot(probs[1][PAIR:WIDE], go[pairs[1], g_at])
            dkv[high, h * 256:h * 256 + DIM] = dk[:, 0:DIM].astype(BF16)
            dkv[high, h * 256 + DIM:(h + 1) * 256] = dv.astype(BF16)
            rot_high = rot_high + dk[:, DIM:256]
        dkr[low, :] = rot_low
        dkr[high, :] = rot_high

    def d_places():
        wide = pl.ds(pl.multiple_of(group * 512, 512), 512)
        thin = pl.ds(pl.multiple_of(group * 256, 256), 256)
        return o_qn.at[:, wide], o_qr.at[:, thin]

    def d_copies(xs):
        target = device(zh, y, s, xs, z)
        at = rows(xs)
        wide, thin = d_places()
        return [
            remote(dqn.at[at], wide, d_send.at[0, xs], d_recv.at[0, group], target),
            remote(dqr.at[at], thin, d_send.at[1, xs], d_recv.at[1, group], target),
        ]

    def d_local():
        at = rows(x)
        wide, thin = d_places()
        return [
            pltpu.make_async_copy(dqn.at[at], wide, loc.at[5]),
            pltpu.make_async_copy(dqr.at[at], thin, loc.at[6]),
        ]

    d_self = [(xs == x) & (s == c) for xs in range(4)]

    def send_queries():
        for t in (0, 1):
            rots = []
            for h in range(GROUP):
                dq = SCALE * dqt[h, t].T
                dqn[pairs[t], h * DIM:(h + 1) * DIM] = dq[:, 0:DIM].astype(BF16)
                rots.append(dq[:, DIM:256])
            for half in (0, 1):
                both = jnp.where(lane < ROPE, rots[2 * half], rots[2 * half + 1])
                dqr[pairs[t], half * 128:(half + 1) * 128] = both.astype(BF16)
        for xs in range(4):
            @pl.when(jnp.logical_not(d_self[xs]))
            def _():
                for copy in d_copies(xs):
                    copy.start()

            @pl.when(d_self[xs])
            def _():
                for copy in d_local():
                    copy.start()

    def y_copy(d):
        peer = (y + d) % 4
        return remote(
            wp.at[:, pl.ds(pl.multiple_of(peer * 256, 256), 256)], yin.at[d - 1],
            y_send.at[d - 1], y_recv.at[d - 1], device(zh, peer, c, x, z),
        )

    def send_weights():
        for n in range(GROUP):
            wp[:, n * 256:(n + 1) * 256] = dot(latt[...], dkv[:, n * 256:(n + 1) * 256]).astype(BF16)
        for d in (2, 1, 3):
            y_copy(d).start()

    def s_copy(k, p):
        return remote(dkp.at[key_rows(p, k, 1 - c)], sin.at[p, k], s_send.at[k, p], s_recv.at[k, p], sib)

    def z_copy(k, p):
        return remote(
            acc.at[p, k, pl.ds(0, HALF)], zin.at[p - 1, k],
            z_send.at[k, p - 1], z_recv.at[k, p - 1], device(zh, y, c, x, across(z, p)),
        )

    def x_copy(k, p):
        return remote(
            acc.at[p, k, pl.ds(HALF, HALF)], xin.at[p, x % 2],
            x_send.at[k, p], x_recv.at[x % 2, p], device(zh, y, s, c + 2 * k, z),
        )

    def x_local(k, p):
        return pltpu.make_async_copy(acc.at[p, k, pl.ds(HALF, HALF)], xin.at[p, x % 2], x_loc.at[p])

    h_self = [(c + 2 * k == x) & (s == c) for k in (0, 1)]

    def join(p):
        for k in (0, 1):
            s_copy(k, p).wait_recv()
            acc[p, k] = (dkp[key_rows(p, k, c), :].astype(F32) + sin[p, k].astype(F32)).astype(BF16)

            @pl.when(jnp.logical_not(h_self[k]))
            def _():
                x_copy(k, p).start()

            @pl.when(h_self[k])
            def _():
                x_local(k, p).start()

    def back(q, carry):
        p = 3 - q
        grads(p)
        at = wide_rows(p)
        dkp[at, 0:LATENT] = dot_bt(dkv[at, :], w[...]).astype(BF16)
        rot = dkr[at, :]
        dkp[at, LATENT:KEYS] = (rot + pltpu.roll(rot, ROPE, 1)).astype(BF16)
        for k in (0, 1):
            s_copy(k, p).start()

        @pl.when(q > 0)
        def _():
            join(p + 1)
            for k in (0, 1):
                z_copy(k, p + 1).start()
        return carry

    lax.fori_loop(0, 4, back, 0)
    send_weights()
    send_queries()
    join(0)

    def zf_copy(p):
        return remote(xsum.at[p - 1], zfin.at[p - 1], zf_send.at[p - 1], zf_recv.at[p - 1], device(zh, y, c, x, across(z, p)))

    def x_total(p):
        for t in (0, 1):
            self_here = (2 * c + t == x) & (x % 2 == c)

            @pl.when(jnp.logical_not(self_here))
            def _():
                remote(acc.at[p, 0, pl.ds(HALF, HALF)], xin.at[p, t], x_send.at[0, p], x_recv.at[t, p], sib).wait_recv()

            @pl.when(self_here)
            def _():
                x_local(0, p).wait()
        return xin[p, 0].astype(F32) + xin[p, 1].astype(F32)

    for p in (3, 2, 1):
        xsum[p - 1] = x_total(p).astype(BF16)
        zf_copy(p).start()
    second = x_total(0)

    for d in (1, 3, 2):
        y_copy(d).wait_recv()
    mine = wp[:, pl.ds(pl.multiple_of(y * 256, 256), 256)].astype(F32)
    ys[...] = (mine + yin[0].astype(F32) + yin[1].astype(F32) + yin[2].astype(F32)).astype(BF16)

    def c_copy(dx, dz):
        px, pz = (x + dx) % 4, (z + dz) % 4
        src = ys.at[pl.ds(pl.multiple_of((4 * px + pz) * 32, 32), 32)]
        return remote(src, cin.at[dx, dz], c_send.at[dx, dz], c_recv.at[dx, dz], device(zh, y, c, px, pz))

    mates = [(dx, dz) for dz in (2, 1, 3, 0) for dx in (2, 1, 3, 0) if dx or dz]
    for dx, dz in mates:
        c_copy(dx, dz).start()

    def h_copy(k):
        return remote(fin.at[k], hin.at[x % 2], h_send.at[k], h_recv.at[x % 2], device(zh, y, s, c + 2 * k, z))

    def h_local(k):
        return pltpu.make_async_copy(fin.at[k], hin.at[x % 2], loc.at[7])

    for k in (0, 1):
        total = acc[0, k, 0:HALF, :].astype(F32)
        for p in (3, 2, 1):
            z_copy(k, p).wait_recv()
            total = total + zin[p - 1, k].astype(F32)
        fin[k] = total.astype(BF16)

        @pl.when(jnp.logical_not(h_self[k]))
        def _():
            h_copy(k).start()

        @pl.when(h_self[k])
        def _():
            h_local(k).start()

    for dx, dz in mates:
        c_copy(dx, dz).wait_recv()
    own = ys[pl.ds(pl.multiple_of((4 * x + z) * 32, 32), 32), :].astype(F32)
    even = own
    for dz in (1, 2, 3):
        even = even + cin[0, dz].astype(F32)
    for dz in range(4):
        even = even + cin[2, dz].astype(F32)
    odd = jnp.zeros_like(own)
    for dx in (1, 3):
        for dz in range(4):
            odd = odd + cin[dx, dz].astype(F32)
    flip = x % 2 == 1
    cs[:, 0:256] = jnp.where(flip, odd, even).astype(BF16)
    cs[:, 256:512] = jnp.where(flip, even, odd).astype(BF16)
    hi_copy = remote(cs, hi_in, hi_sem.at[0], hi_sem.at[1], device(1 - zh, y, c, x, z))
    hi_copy.start()

    for t in (0, 1):
        self_here = (2 * c + t == x) & (x % 2 == c)

        @pl.when(jnp.logical_not(self_here))
        def _():
            remote(fin.at[0], hin.at[t], h_send.at[0], h_recv.at[t], sib).wait_recv()
    for k in (0, 1):
        @pl.when(h_self[k])
        def _():
            h_local(k).wait()
    for p in (1, 2, 3):
        zf_copy(p).wait_recv()
        second = second + zfin[p - 1].astype(F32)
    final = jnp.concatenate([hin[0].astype(F32) + hin[1].astype(F32), second], axis=0)
    o_lat[...] = final[:, 0:LATENT].astype(BF16)
    o_rot[...] = final[:, LATENT:KEYS].T[0:ROPE, :].astype(BF16)

    hi_copy.wait_recv()
    fs[...] = (cs[...].astype(F32) + hi_in[...].astype(F32)).astype(BF16)

    def a_copy(dy, dc):
        peer = device(zh, (y + dy) % 4, (c + dc) % 2, x, z)
        return remote(fs, ag.at[dy, dc], a_send.at[dy, dc], a_recv.at[dy, dc], peer)

    members = [(dy, dc) for dy in (2, 1, 3, 0) for dc in (0, 1) if dy or dc]
    for dy, dc in members:
        a_copy(dy, dc).start()

    def place(values, from_y, from_c):
        wide = values.astype(F32)
        for parity in (0, 1):
            at = pl.multiple_of((2 * parity + from_c) * 1024 + from_y * 256, 256)
            o_w[:, pl.ds(at, 256)] = wide[:, parity * 256:(parity + 1) * 256]

    place(fs[...], y, c)
    for dy, dc in members:
        a_copy(dy, dc).wait_recv()
        place(ag[dy, dc], (y + 4 - dy) % 4, (c + dc) % 2)

    for gs in range(4):
        self_here = (group == gs) & (s == c)

        @pl.when(jnp.logical_not(self_here))
        def _():
            remote(dqn.at[0:BLOCK], o_qn.at[:, gs * 512:(gs + 1) * 512], d_send.at[0, 0], d_recv.at[0, gs], sib).wait_recv()
            remote(dqr.at[0:BLOCK], o_qr.at[:, gs * 256:(gs + 1) * 256], d_send.at[1, 0], d_recv.at[1, gs], sib).wait_recv()

    for t in (0, 1):
        @pl.when(jnp.logical_not(key_self[t]))
        def _():
            key_send(t).wait_send()
    for g in range(4):
        @pl.when(jnp.logical_not(q_self[g]))
        def _():
            for copy in q_copies(g, sib):
                copy.wait_send()
    lens_copy.wait_send()
    for k in (0, 1):
        for p in (1, 2, 3):
            z_key(k, p).wait_send()
            z_copy(k, p).wait_send()
        for p in range(4):
            sib_key(k, p, c).wait_send()
            s_copy(k, p).wait_send()

        @pl.when(jnp.logical_not(h_self[k]))
        def _():
            h_copy(k).wait_send()
    for p in (1, 2, 3):
        zs_copy(p).wait_send()
        zf_copy(p).wait_send()
        for t in (0, 1):
            @pl.when(jnp.logical_not(key_self[t]))
            def _():
                kf_copy(t, p).wait_send()
    for k in (0, 1):
        for p in range(4):
            @pl.when(jnp.logical_not(h_self[k]))
            def _():
                x_copy(k, p).wait_send()
    for xs in range(4):
        @pl.when(jnp.logical_not(d_self[xs]))
        def _():
            for copy in d_copies(xs):
                copy.wait_send()

        @pl.when(d_self[xs])
        def _():
            for copy in d_local():
                copy.wait()
    for d in (1, 2, 3):
        y_copy(d).wait_send()
    for dx, dz in mates:
        c_copy(dx, dz).wait_send()
    hi_copy.wait_send()
    for dy, dc in members:
        a_copy(dy, dc).wait_send()


def shape(dims, kind=BF16):
    return jax.ShapeDtypeStruct(dims, kind)


def dma(*dims):
    return pltpu.SemaphoreType.DMA(dims)


def finish_kernel(*refs):
    sems = refs[15]
    into = [pltpu.make_async_copy(refs[i], refs[10 + i], sems.at[0, i]) for i in range(5)]
    out = [pltpu.make_async_copy(refs[10 + i], refs[5 + i], sems.at[1, i]) for i in range(5)]
    for copy in into:
        copy.start()
    for i in range(5):
        into[i].wait()
        out[i].start()
    for copy in out:
        copy.wait()


def body(query_nope, query_rope, latent, key_rope, grad_output, kv_up, doc_lengths):
    here = pl.BlockSpec(memory_space=pltpu.VMEM)
    outs = pl.pallas_call(
        kernel,
        name="whole_rows",
        out_shape=(
            shape((BLOCK, HEADS * DIM)),
            shape((BLOCK, HEADS * ROPE)),
            shape((BLOCK, LATENT)),
            shape((ROPE, BLOCK)),
            shape((32, HEADS * 256), F32),
        ),
        in_specs=[here] * 6 + [pl.BlockSpec(memory_space=pl.ANY)],
        out_specs=(here,) * 5,
        scratch_shapes=[
            VMEM((BLOCK, KEYS), BF16),
            VMEM((LATENT, GROUP * 256), BF16),
            VMEM((WIDE, GROUP * DIM), BF16),
            VMEM((WIDE, GROUP * DIM), BF16),
            VMEM((WIDE, GROUP * ROPE), BF16),
            VMEM((8, 128), jnp.int32),
            VMEM((8, 128), jnp.int32),
            VMEM((SEQ, KEYS), BF16),
            VMEM((3, HALF, KEYS), BF16),
            VMEM((SEQ, GROUP * 256), BF16),
            VMEM((SEQ, GROUP * DIM), BF16),
            VMEM((GROUP, 256, SEQ), BF16),
            VMEM((WIDE, GROUP * 256), BF16),
            VMEM((GROUP, 4 * PAIR, PAIR), F32),
            VMEM((GROUP, 4 * WIDE, PAIR), F32),
            VMEM((GROUP, 2, 3, 8, PAIR), F32),
            VMEM((SEQ, GROUP * 256), BF16),
            VMEM((SEQ, 128), F32),
            VMEM((GROUP, 2, 256, PAIR), F32),
            VMEM((LATENT, SEQ), BF16),
            VMEM((WIDE, GROUP * DIM), BF16),
            VMEM((WIDE, GROUP * ROPE), BF16),
            VMEM((LATENT, GROUP * 256), BF16),
            VMEM((SEQ, KEYS), BF16),
            VMEM((4, 2, BLOCK, KEYS), BF16),
            VMEM((4, 2, BLOCK, KEYS), BF16),
            VMEM((3, 2, HALF, KEYS), BF16),
            VMEM((2, HALF, KEYS), BF16),
            VMEM((2, HALF, KEYS), BF16),
            VMEM((4, 2, HALF, KEYS), BF16),
            VMEM((3, HALF, KEYS), BF16),
            VMEM((3, HALF, KEYS), BF16),
            VMEM((3, LATENT, 256), BF16),
            VMEM((LATENT, 256), BF16),
            VMEM((4, 4, 32, 256), BF16),
            VMEM((32, 512), BF16),
            VMEM((32, 512), BF16),
            VMEM((32, 512), BF16),
            VMEM((4, 2, 32, 512), BF16),
            dma(3, 4), dma(3, 4), dma(2), dma(2), dma(2, 3), dma(2, 3), dma(2, 4), dma(2, 4), dma(2), dma(8),
            dma(3), dma(3), dma(2, 3), dma(2, 3), dma(3),
            dma(2, 4), dma(2, 4), dma(2, 4), dma(2, 4), dma(2, 3), dma(2, 3), dma(2), dma(2),
            dma(2, 4), dma(2, 4), dma(4), dma(3), dma(3),
            dma(3), dma(3), dma(4, 4), dma(4, 4), dma(2), dma(4, 2), dma(4, 2),
        ],
        compiler_params=pltpu.CompilerParams(collective_id=0, has_side_effects=True, vmem_limit_bytes=58 * MIB),
    )(query_nope[0], query_rope[0], grad_output[0], latent[0], key_rope[0].T, doc_lengths, kv_up)
    anywhere = pl.BlockSpec(memory_space=pl.ANY)
    gqn, gqr, glat, grot, gw = pl.pallas_call(
        finish_kernel,
        name="finish_rows",
        out_shape=[shape(out.shape, out.dtype) for out in outs],
        in_specs=[anywhere] * 5,
        out_specs=[anywhere] * 5,
        scratch_shapes=[VMEM(out.shape, out.dtype) for out in outs] + [dma(2, 5)],
    )(*outs)
    return gqn[None], gqr[None], glat[None], grot.T[None], gw


def solution(mesh):
    rows = P("dp", "ctx", None)
    return jax.shard_map(
        body,
        mesh=mesh,
        in_specs=(rows, rows, rows, rows, rows, P(), P("dp", None)),
        out_specs=(rows, rows, rows, rows, P("ctx", None)),
        check_vma=False,
    )
```

```python
import functools
import math

import jax
import jax.numpy as jnp
from jax import lax
from jax.experimental import pallas as pl
from jax.experimental.pallas import tpu as pltpu
from jax.sharding import PartitionSpec as P

HEADS = 16
DIM = 128
ROPE = 64
LATENT = 512
BLOCK = 128
SEQ = 2048
GROUP = 4
SCALE = (DIM + ROPE) ** -0.5
NEGATIVE = -1e30
MESH = pl.DeviceIdType.MESH
VMEM = pltpu.VMEM
F32 = jnp.float32
BF16 = jnp.bfloat16
MIB = 1 << 20


def coords():
    dp, ctx = lax.axis_index("dp"), lax.axis_index("ctx")
    return dp // 8, (dp // 2) % 4, dp % 2, ctx // 4, ctx % 4


def device(zh, y, c, x, z):
    return ((zh * 4 + y) * 2 + c, x * 4 + z)


def remote(src, dst, send, recv, target):
    return pltpu.make_async_remote_copy(
        src_ref=src, dst_ref=dst, send_sem=send, recv_sem=recv, device_id=target, device_id_type=MESH
    )


def greet(targets):
    barrier = pltpu.get_barrier_semaphore()
    for target in targets:
        pl.semaphore_signal(barrier, inc=1, device_id=target, device_id_type=MESH)
    pl.semaphore_wait(barrier, len(targets))


def dot_bt(left, right):
    return lax.dot_general(left, right, (((1,), (1,)), ((), ())), preferred_element_type=F32)


def dot(left, right):
    return jnp.dot(left, right, preferred_element_type=F32)


PAIR = 2 * BLOCK
WIDE = 4 * BLOCK
KEYS = LATENT + 2 * ROPE


def fold(values, op):
    return op(values.reshape(values.shape[0] // 8, 8, values.shape[1]), axis=0)


def across(a, p):
    return (a % 2 + p % 2) % 2 + 2 * ((a // 2 + p // 2) % 2)


def kernel(
    nope, rope, gout, lat, krope, lens, kv_up,
    o_qn, o_qr, o_lat, o_rot, o_w,
    kblk, w, qn, go, qr, own_lens, other_lens, keys, zstage,
    kx, vx, ktx, qx, st0, st1, stats, dkv, dkr, dqt, latt, dqn, dqr, wp,
    dkp, sin, acc, zin, fin, hin, xin, xsum, zfin, yin, ys, cin, cs, hi_in, fs, ag,
    q_send, q_recv, kx_send, kx_recv, kz_send, kz_recv, ks_send, ks_recv, l_sem, loc,
    zs_sem, kf_send, kf_recv,
    d_send, d_recv, s_send, s_recv, z_send, z_recv, h_send, h_recv, x_send, x_recv, x_loc, zf_send, zf_recv,
    y_send, y_recv, c_send, c_recv, hi_sem, a_send, a_recv,
):
    zh, y, c, x, z = coords()
    s = x // 2
    group = 2 * (x % 2) + c
    sib = device(zh, y, 1 - c, x, z)
    others = [device(zh, y, c, (x + dx) % 4, (z + dz) % 4) for dx in range(4) for dz in range(4) if dx or dz]
    others += [device(zh, y, 1 - c, (x + d) % 4, z) for d in range(4)]
    others += [device(zh, (y + d) % 4, cc, x, z) for d in (1, 2, 3) for cc in (0, 1)]
    others += [device(1 - zh, y, c, x, z)]
    lane = lax.broadcasted_iota(jnp.int32, (1, 2 * ROPE), 1)

    def rows(at, size=BLOCK):
        return pl.ds(pl.multiple_of(at * BLOCK, BLOCK), size)

    def wide_rows(p):
        return pl.ds(pl.multiple_of(p * WIDE, WIDE), WIDE)

    w_copy = pltpu.make_async_copy(kv_up.at[:, pl.ds(pl.multiple_of(group * 1024, 1024), 1024)], w, loc.at[4])
    w_copy.start()
    kblk[:, 0:LATENT] = lat[...]
    pair = krope[...].T
    own_lens[...] = jnp.zeros(own_lens.shape, jnp.int32)
    own_lens[0:1, 0:8] = lens[...]
    kblk[:, LATENT:KEYS] = jnp.concatenate([pair, pair], axis=1)
    greet(others)

    def key_send(t):
        return remote(kblk, keys.at[rows(x)], kx_send.at[t], kx_recv.at[x // 2], device(zh, y, x % 2, 2 * c + t, z))

    def key_local():
        return pltpu.make_async_copy(kblk, keys.at[rows(x)], loc.at[0])

    key_self = [(2 * c + t == x) & (x % 2 == c) for t in (0, 1)]
    for t in (0, 1):
        @pl.when(jnp.logical_not(key_self[t]))
        def _():
            key_send(t).start()

        @pl.when(key_self[t])
        def _():
            key_local().start()

    def zs_copy():
        return remote(kblk, zstage, zs_sem.at[0], zs_sem.at[1], device(zh, y, c, x, across(z, 3)))

    zs_copy().start()

    def q_copies(g, target):
        wide = pl.ds(g * GROUP * DIM, GROUP * DIM)
        thin = pl.ds(g * GROUP * ROPE, GROUP * ROPE)
        return [
            remote(nope.at[:, wide], qn.at[rows(x)], q_send.at[0, g], q_recv.at[0, x], target),
            remote(rope.at[:, thin], qr.at[rows(x)], q_send.at[2, g], q_recv.at[2, x], target),
            remote(gout.at[:, wide], go.at[rows(x)], q_send.at[1, g], q_recv.at[1, x], target),
        ]

    def q_local(g):
        wide = pl.ds(g * GROUP * DIM, GROUP * DIM)
        thin = pl.ds(g * GROUP * ROPE, GROUP * ROPE)
        return [
            pltpu.make_async_copy(nope.at[:, wide], qn.at[rows(x)], loc.at[1]),
            pltpu.make_async_copy(gout.at[:, wide], go.at[rows(x)], loc.at[2]),
            pltpu.make_async_copy(rope.at[:, thin], qr.at[rows(x)], loc.at[3]),
        ]

    q_self = [(2 * c + g // 2 == x) & (c == g % 2) for g in range(4)]
    for g in range(4):
        @pl.when(jnp.logical_not(q_self[g]))
        def _():
            for copy in q_copies(g, device(zh, y, g % 2, 2 * c + g // 2, z)):
                copy.start()

        @pl.when(q_self[g])
        def _():
            for copy in q_local(g):
                copy.start()

    lens_copy = remote(own_lens, other_lens, l_sem.at[0], l_sem.at[1], sib)
    lens_copy.start()

    def key_rows(p, k, core):
        return rows(4 * p + core + 2 * k)

    def z_key(k, p):
        return remote(
            keys.at[key_rows(0, k, c)], keys.at[key_rows(p, k, c)],
            kz_send.at[k, p - 1], kz_recv.at[k, p - 1], device(zh, y, c, x, across(z, p)),
        )

    def kf_copy(t):
        return remote(
            zstage, keys.at[key_rows(3, x // 2, x % 2)],
            kf_send.at[t], kf_recv.at[x // 2], device(zh, y, x % 2, 2 * c + t, z),
        )

    def kf_local():
        return pltpu.make_async_copy(zstage, keys.at[key_rows(3, x // 2, x % 2)], loc.at[0])

    def sib_key(k, p, core):
        at = key_rows(p, k, core)
        return remote(keys.at[at], keys.at[at], ks_send.at[k, p], ks_recv.at[k, p], sib)

    for k in (0, 1):
        own = c + 2 * k
        self_here = (own == x) & (s == c)

        @pl.when(jnp.logical_not(self_here))
        def _():
            remote(kblk, keys.at[rows(own)], kx_send.at[0], kx_recv.at[k], sib).wait_recv()

        @pl.when(self_here)
        def _():
            key_local().wait()

        for p in (1, 2):
            z_key(k, p).start()
        sib_key(k, 0, c).start()

    def take(p):
        for k in (0, 1):
            sib_key(k, p, 1 - c).wait_recv()

    def pass_on(p):
        for k in (0, 1):
            z_key(k, p).wait_recv()
            sib_key(k, p, c).start()

    def pass_last():
        for k in (0, 1):
            self_here = (c + 2 * k == x) & (s == c)

            @pl.when(jnp.logical_not(self_here))
            def _():
                remote(zstage, keys.at[key_rows(3, k, c)], kf_send.at[0], kf_recv.at[k], sib).wait_recv()

            @pl.when(self_here)
            def _():
                kf_local().wait()

            sib_key(k, 3, c).start()

    w_copy.wait()
    wt = [w[:, h * 256:h * 256 + DIM].T for h in range(GROUP)]

    def project(p):
        at = wide_rows(p)
        own = keys[at, 0:LATENT]
        rot = keys[at, LATENT:KEYS]
        rot_t = rot.T
        for h in range(GROUP):
            both = dot(own, w[:, h * 256:(h + 1) * 256]).astype(BF16)
            kx[at, h * 256:h * 256 + DIM] = both[:, 0:DIM]
            kx[at, h * 256 + DIM:(h + 1) * 256] = rot
            vx[at, h * DIM:(h + 1) * DIM] = both[:, DIM:256]
            ktx[h, 0:DIM, at] = dot_bt(wt[h], own).astype(BF16)
            ktx[h, DIM:256, at] = rot_t
        latt[:, at] = own.T

    def first(p, carry):
        @pl.when(p == 1)
        def _():
            zs_copy().wait_recv()
            for t in (0, 1):
                @pl.when(jnp.logical_not(key_self[t]))
                def _():
                    kf_copy(t).start()

                @pl.when(key_self[t])
                def _():
                    kf_local().start()
            pass_on(1)

        take(p)
        project(p)
        return carry

    lax.fori_loop(0, 2, first, 0)

    lens_copy.wait_recv()
    sizes = jnp.where(s == c, own_lens[0:1, :], other_lens[0:1, :])
    row_lane = lax.broadcasted_iota(jnp.int32, (1, PAIR), 1)
    positions, starts = [], []
    for t in (0, 1):
        pos = (4 * (2 * t + row_lane // BLOCK) + z) * BLOCK + row_lane % BLOCK
        start = jnp.zeros_like(pos)
        end = jnp.zeros_like(sizes[:, 0:1])
        for d in range(8):
            end = end + sizes[:, d:d + 1]
            start = jnp.maximum(start, jnp.where(end <= pos, end, 0))
        positions.append(pos)
        starts.append(start)
    stats[...] = jnp.zeros(stats.shape, F32)
    for h in range(GROUP):
        for t in (0, 1):
            stats[h, t, 0] = jnp.full((8, PAIR), NEGATIVE, F32)
    dqt[...] = jnp.zeros(dqt.shape, F32)

    for xs in range(4):
        self_here = (xs == x) & (s == c)

        @pl.when(jnp.logical_not(self_here))
        def _():
            at = rows(xs)
            remote(nope.at[:, 0:GROUP * DIM], qn.at[at], q_send.at[0, 0], q_recv.at[0, xs], sib).wait_recv()
            remote(rope.at[:, 0:GROUP * ROPE], qr.at[at], q_send.at[2, 0], q_recv.at[2, xs], sib).wait_recv()
            remote(gout.at[:, 0:GROUP * DIM], go.at[at], q_send.at[1, 0], q_recv.at[1, xs], sib).wait_recv()
    for g in range(4):
        @pl.when(q_self[g])
        def _():
            for copy in q_local(g):
                copy.wait()
    for h in range(GROUP):
        qx[:, h * 256:h * 256 + DIM] = qn[:, h * DIM:(h + 1) * DIM]
        half = qr[:, (h // 2) * 128:(h // 2) * 128 + 128]
        keep = (lane < ROPE) if h % 2 == 0 else (lane >= ROPE)
        qx[:, h * 256 + DIM:(h + 1) * 256] = jnp.where(keep, half, jnp.zeros_like(half))

    pairs = [slice(0, PAIR), slice(PAIR, WIDE)]
    spans = [PAIR, WIDE]
    scores = [st0, st1]

    def span(p, t):
        return pl.ds(pl.multiple_of(p * spans[t], spans[t]), spans[t])

    def key_span(p, t):
        return pl.ds(pl.multiple_of(p * WIDE, WIDE), spans[t])

    def look(p):
        base = lax.broadcasted_iota(jnp.int32, (WIDE, 1), 0)
        key = base + (base // BLOCK) * (3 * BLOCK) + across(z, p) * BLOCK
        for t in (0, 1):
            part = key[0:spans[t]]
            seen = (part <= positions[t]) & (part >= starts[t])
            for h in range(GROUP):
                at = key_span(p, t)
                v = dot_bt(kx[at, h * 256:(h + 1) * 256], qx[pairs[t], h * 256:(h + 1) * 256])
                d = dot_bt(vx[at, h * DIM:(h + 1) * DIM], go[pairs[t], h * DIM:(h + 1) * DIM])
                v = jnp.where(seen, v * (SCALE * math.log2(math.e)), NEGATIVE)
                scores[t][h, span(p, t), :] = v
                old = stats[h, t, 0]
                top = jnp.maximum(old, fold(v, jnp.max))
                e = jnp.exp2(v.reshape(spans[t] // 8, 8, PAIR) - top[None])
                factor = jnp.exp2(old - top)
                stats[h, t, 0] = top
                stats[h, t, 1] = stats[h, t, 1] * factor + jnp.sum(e, axis=0)
                stats[h, t, 2] = stats[h, t, 2] * factor + jnp.sum(e * d.reshape(spans[t] // 8, 8, PAIR), axis=0)

    def early(p, carry):
        look(p)

        @pl.when(p == 0)
        def _():
            pass_on(2)

        return carry

    def late(p, carry):
        take(p)
        project(p)

        @pl.when(p == 2)
        def _():
            pass_last()

        look(p)
        return carry

    lax.fori_loop(0, 2, early, 0)
    lax.fori_loop(2, 4, late, 0)

    logs, inners = [], []
    for h in range(GROUP):
        for t in (0, 1):
            top8 = stats[h, t, 0]
            top = jnp.max(top8, axis=0, keepdims=True)
            factor = jnp.exp2(top8 - top)
            total = jnp.sum(stats[h, t, 1] * factor, axis=0, keepdims=True)
            inners.append(jnp.sum(stats[h, t, 2] * factor, axis=0, keepdims=True) / total)
            logs.append(top + jnp.log2(total))

    def grads(p):
        at = wide_rows(p)
        low = pl.ds(pl.multiple_of(p * WIDE, WIDE), PAIR)
        high = pl.ds(pl.multiple_of(p * WIDE + PAIR, PAIR), PAIR)
        rot_low = jnp.zeros((PAIR, 2 * ROPE), F32)
        rot_high = jnp.zeros((PAIR, 2 * ROPE), F32)
        for h in range(GROUP):
            probs, diffs = [], []
            for t in (0, 1):
                e = jnp.exp2(scores[t][h, span(p, t), :] - logs[2 * h + t])
                d = dot_bt(vx[key_span(p, t), h * DIM:(h + 1) * DIM], go[pairs[t], h * DIM:(h + 1) * DIM])
                diff = (e * (d - inners[2 * h + t])).astype(BF16)
                dqt[h, t] += dot(ktx[h, :, key_span(p, t)], diff)
                probs.append(e.astype(BF16))
                diffs.append(diff)
            q_at, g_at = slice(h * 256, (h + 1) * 256), slice(h * DIM, (h + 1) * DIM)
            dk = SCALE * dot(jnp.concatenate([diffs[0], diffs[1][0:PAIR]], axis=1), qx[:, q_at])
            dv = dot(jnp.concatenate([probs[0], probs[1][0:PAIR]], axis=1), go[:, g_at])
            dkv[low, h * 256:h * 256 + DIM] = dk[:, 0:DIM].astype(BF16)
            dkv[low, h * 256 + DIM:(h + 1) * 256] = dv.astype(BF16)
            rot_low = rot_low + dk[:, DIM:256]
            dk = SCALE * dot(diffs[1][PAIR:WIDE], qx[pairs[1], q_at])
            dv = dot(probs[1][PAIR:WIDE], go[pairs[1], g_at])
            dkv[high, h * 256:h * 256 + DIM] = dk[:, 0:DIM].astype(BF16)
            dkv[high, h * 256 + DIM:(h + 1) * 256] = dv.astype(BF16)
            rot_high = rot_high + dk[:, DIM:256]
        dkr[low, :] = rot_low
        dkr[high, :] = rot_high

    def d_places():
        wide = pl.ds(pl.multiple_of(group * 512, 512), 512)
        thin = pl.ds(pl.multiple_of(group * 256, 256), 256)
        return o_qn.at[:, wide], o_qr.at[:, thin]

    def d_copies(xs):
        target = device(zh, y, s, xs, z)
        at = rows(xs)
        wide, thin = d_places()
        return [
            remote(dqn.at[at], wide, d_send.at[0, xs], d_recv.at[0, group], target),
            remote(dqr.at[at], thin, d_send.at[1, xs], d_recv.at[1, group], target),
        ]

    def d_local():
        at = rows(x)
        wide, thin = d_places()
        return [
            pltpu.make_async_copy(dqn.at[at], wide, loc.at[5]),
            pltpu.make_async_copy(dqr.at[at], thin, loc.at[6]),
        ]

    d_self = [(xs == x) & (s == c) for xs in range(4)]

    def send_queries():
        for t in (0, 1):
            rots = []
            for h in range(GROUP):
                dq = SCALE * dqt[h, t].T
                dqn[pairs[t], h * DIM:(h + 1) * DIM] = dq[:, 0:DIM].astype(BF16)
                rots.append(dq[:, DIM:256])
            for half in (0, 1):
                both = jnp.where(lane < ROPE, rots[2 * half], rots[2 * half + 1])
                dqr[pairs[t], half * 128:(half + 1) * 128] = both.astype(BF16)
        for xs in range(4):
            @pl.when(jnp.logical_not(d_self[xs]))
            def _():
                for copy in d_copies(xs):
                    copy.start()

            @pl.when(d_self[xs])
            def _():
                for copy in d_local():
                    copy.start()

    def y_copy(d):
        peer = (y + d) % 4
        return remote(
            wp.at[:, pl.ds(pl.multiple_of(peer * 256, 256), 256)], yin.at[d - 1],
            y_send.at[d - 1], y_recv.at[d - 1], device(zh, peer, c, x, z),
        )

    def send_weights():
        for n in range(GROUP):
            wp[:, n * 256:(n + 1) * 256] = dot(latt[...], dkv[:, n * 256:(n + 1) * 256]).astype(BF16)

            @pl.when(y != n)
            def _():
                slot = (n + 3 - y) % 4
                remote(
                    wp.at[:, pl.ds(n * 256, 256)], yin.at[slot], y_send.at[slot], y_recv.at[slot], device(zh, n, c, x, z)
                ).start()

    def s_copy(k, p):
        return remote(dkp.at[key_rows(p, k, 1 - c)], sin.at[p, k], s_send.at[k, p], s_recv.at[k, p], sib)

    def z_copy(k):
        return remote(acc.at[1, k], zin.at[k], z_send.at[k], z_recv.at[k], device(zh, y, c, x, across(z, 1)))

    def x_copy(k, p):
        return remote(
            acc.at[p, k], xin.at[p - 2, x % 2],
            x_send.at[k, p - 2], x_recv.at[x % 2, p - 2], device(zh, y, s, c + 2 * k, z),
        )

    def x_local(k, p):
        return pltpu.make_async_copy(acc.at[p, k], xin.at[p - 2, x % 2], x_loc.at[p - 2])

    h_self = [(c + 2 * k == x) & (s == c) for k in (0, 1)]

    def join(p):
        for k in (0, 1):
            s_copy(k, p).wait_recv()
            acc[p, k] = (dkp[key_rows(p, k, c), :].astype(F32) + sin[p, k].astype(F32)).astype(BF16)

    def send_join(p):
        for k in (0, 1):
            @pl.when(jnp.logical_not(h_self[k]))
            def _():
                x_copy(k, p).start()

            @pl.when(h_self[k])
            def _():
                x_local(k, p).start()

    def back(q, carry):
        p = 3 - q
        grads(p)
        at = wide_rows(p)
        dkp[at, 0:LATENT] = dot_bt(dkv[at, :], w[...]).astype(BF16)
        rot = dkr[at, :]
        dkp[at, LATENT:KEYS] = (rot + pltpu.roll(rot, ROPE, 1)).astype(BF16)
        for k in (0, 1):
            s_copy(k, p).start()

        @pl.when(q > 0)
        def _():
            join(p + 1)

        @pl.when((q == 1) | (q == 2))
        def _():
            send_join(p + 1)

        @pl.when(q == 3)
        def _():
            for k in (0, 1):
                z_copy(k).start()
        return carry

    lax.fori_loop(0, 4, back, 0)
    send_weights()
    join(0)

    def zf_copy(p):
        return remote(xsum.at[p - 2], zfin.at[p - 2], zf_send.at[p - 2], zf_recv.at[p - 2], device(zh, y, c, x, across(z, p)))

    for p in (3, 2):
        for t in (0, 1):
            self_here = (2 * c + t == x) & (x % 2 == c)

            @pl.when(jnp.logical_not(self_here))
            def _():
                remote(acc.at[p, 0], xin.at[p - 2, t], x_send.at[0, p - 2], x_recv.at[t, p - 2], sib).wait_recv()

            @pl.when(self_here)
            def _():
                x_local(0, p).wait()
        xsum[p - 2] = (xin[p - 2, 0].astype(F32) + xin[p - 2, 1].astype(F32)).astype(BF16)
        zf_copy(p).start()

    send_queries()

    for d in (1, 3, 2):
        y_copy(d).wait_recv()
    mine = wp[:, pl.ds(pl.multiple_of(y * 256, 256), 256)].astype(F32)
    ys[...] = (mine + yin[0].astype(F32) + yin[1].astype(F32) + yin[2].astype(F32)).astype(BF16)

    def c_copy(dx, dz):
        px, pz = (x + dx) % 4, (z + dz) % 4
        src = ys.at[pl.ds(pl.multiple_of((4 * px + pz) * 32, 32), 32)]
        return remote(src, cin.at[dx, dz], c_send.at[dx, dz], c_recv.at[dx, dz], device(zh, y, c, px, pz))

    mates = [(dx, dz) for dz in (2, 1, 3, 0) for dx in (2, 1, 3, 0) if dx or dz]
    for dx, dz in mates:
        c_copy(dx, dz).start()

    def h_copy(k):
        return remote(fin.at[k], hin.at[x % 2], h_send.at[k], h_recv.at[x % 2], device(zh, y, s, c + 2 * k, z))

    def h_local(k):
        return pltpu.make_async_copy(fin.at[k], hin.at[x % 2], loc.at[7])

    for k in (0, 1):
        z_copy(k).wait_recv()
        total = acc[0, k].astype(F32) + zin[k].astype(F32)
        fin[k] = total.astype(BF16)

        @pl.when(jnp.logical_not(h_self[k]))
        def _():
            h_copy(k).start()

        @pl.when(h_self[k])
        def _():
            h_local(k).start()

    for dx, dz in mates:
        c_copy(dx, dz).wait_recv()
    own = ys[pl.ds(pl.multiple_of((4 * x + z) * 32, 32), 32), :].astype(F32)
    even = own
    for dz in (1, 2, 3):
        even = even + cin[0, dz].astype(F32)
    for dz in range(4):
        even = even + cin[2, dz].astype(F32)
    odd = jnp.zeros_like(own)
    for dx in (1, 3):
        for dz in range(4):
            odd = odd + cin[dx, dz].astype(F32)
    flip = x % 2 == 1
    cs[:, 0:256] = jnp.where(flip, odd, even).astype(BF16)
    cs[:, 256:512] = jnp.where(flip, even, odd).astype(BF16)
    hi_copy = remote(cs, hi_in, hi_sem.at[0], hi_sem.at[1], device(1 - zh, y, c, x, z))
    hi_copy.start()

    for t in (0, 1):
        self_here = (2 * c + t == x) & (x % 2 == c)

        @pl.when(jnp.logical_not(self_here))
        def _():
            remote(fin.at[0], hin.at[t], h_send.at[0], h_recv.at[t], sib).wait_recv()
    for k in (0, 1):
        @pl.when(h_self[k])
        def _():
            h_local(k).wait()
    final = hin[0].astype(F32) + hin[1].astype(F32)
    for p in (3, 2):
        zf_copy(p).wait_recv()
        final = final + zfin[p - 2].astype(F32)
    o_lat[...] = final[:, 0:LATENT].astype(BF16)
    o_rot[...] = final[:, LATENT:KEYS].T[0:ROPE, :].astype(BF16)

    hi_copy.wait_recv()
    fs[...] = (cs[...].astype(F32) + hi_in[...].astype(F32)).astype(BF16)

    def a_copy(dy, dc):
        peer = device(zh, (y + dy) % 4, (c + dc) % 2, x, z)
        return remote(fs, ag.at[dy, dc], a_send.at[dy, dc], a_recv.at[dy, dc], peer)

    members = [(dy, dc) for dy in (2, 1, 3, 0) for dc in (0, 1) if dy or dc]
    for dy, dc in members:
        a_copy(dy, dc).start()

    def place(values, from_y, from_c):
        wide = values.astype(F32)
        for parity in (0, 1):
            at = pl.multiple_of((2 * parity + from_c) * 1024 + from_y * 256, 256)
            o_w[:, pl.ds(at, 256)] = wide[:, parity * 256:(parity + 1) * 256]

    place(fs[...], y, c)
    for dy, dc in members:
        a_copy(dy, dc).wait_recv()
        place(ag[dy, dc], (y + 4 - dy) % 4, (c + dc) % 2)

    for gs in range(4):
        self_here = (group == gs) & (s == c)

        @pl.when(jnp.logical_not(self_here))
        def _():
            remote(dqn.at[0:BLOCK], o_qn.at[:, gs * 512:(gs + 1) * 512], d_send.at[0, 0], d_recv.at[0, gs], sib).wait_recv()
            remote(dqr.at[0:BLOCK], o_qr.at[:, gs * 256:(gs + 1) * 256], d_send.at[1, 0], d_recv.at[1, gs], sib).wait_recv()

    for t in (0, 1):
        @pl.when(jnp.logical_not(key_self[t]))
        def _():
            key_send(t).wait_send()
    for g in range(4):
        @pl.when(jnp.logical_not(q_self[g]))
        def _():
            for copy in q_copies(g, sib):
                copy.wait_send()
    lens_copy.wait_send()
    for k in (0, 1):
        for p in (1, 2):
            z_key(k, p).wait_send()
        z_copy(k).wait_send()
        for p in range(4):
            sib_key(k, p, c).wait_send()
            s_copy(k, p).wait_send()

        @pl.when(jnp.logical_not(h_self[k]))
        def _():
            h_copy(k).wait_send()
    zs_copy().wait_send()
    for t in (0, 1):
        @pl.when(jnp.logical_not(key_self[t]))
        def _():
            kf_copy(t).wait_send()
    for p in (3, 2):
        zf_copy(p).wait_send()
        for k in (0, 1):
            @pl.when(jnp.logical_not(h_self[k]))
            def _():
                x_copy(k, p).wait_send()
    for xs in range(4):
        @pl.when(jnp.logical_not(d_self[xs]))
        def _():
            for copy in d_copies(xs):
                copy.wait_send()

        @pl.when(d_self[xs])
        def _():
            for copy in d_local():
                copy.wait()
    for d in (1, 2, 3):
        y_copy(d).wait_send()
    for dx, dz in mates:
        c_copy(dx, dz).wait_send()
    hi_copy.wait_send()
    for dy, dc in members:
        a_copy(dy, dc).wait_send()


def shape(dims, kind=BF16):
    return jax.ShapeDtypeStruct(dims, kind)


def dma(*dims):
    return pltpu.SemaphoreType.DMA(dims)


def finish_kernel(*refs):
    sems = refs[15]
    into = [pltpu.make_async_copy(refs[i], refs[10 + i], sems.at[0, i]) for i in range(5)]
    out = [pltpu.make_async_copy(refs[10 + i], refs[5 + i], sems.at[1, i]) for i in range(5)]
    for copy in into:
        copy.start()
    for i in range(5):
        into[i].wait()
        out[i].start()
    for copy in out:
        copy.wait()


def body(query_nope, query_rope, latent, key_rope, grad_output, kv_up, doc_lengths):
    here = pl.BlockSpec(memory_space=pltpu.VMEM)
    outs = pl.pallas_call(
        kernel,
        name="whole_rows",
        out_shape=(
            shape((BLOCK, HEADS * DIM)),
            shape((BLOCK, HEADS * ROPE)),
            shape((BLOCK, LATENT)),
            shape((ROPE, BLOCK)),
            shape((32, HEADS * 256), F32),
        ),
        in_specs=[here] * 6 + [pl.BlockSpec(memory_space=pl.ANY)],
        out_specs=(here,) * 5,
        scratch_shapes=[
            VMEM((BLOCK, KEYS), BF16),
            VMEM((LATENT, GROUP * 256), BF16),
            VMEM((WIDE, GROUP * DIM), BF16),
            VMEM((WIDE, GROUP * DIM), BF16),
            VMEM((WIDE, GROUP * ROPE), BF16),
            VMEM((8, 128), jnp.int32),
            VMEM((8, 128), jnp.int32),
            VMEM((SEQ, KEYS), BF16),
            VMEM((BLOCK, KEYS), BF16),
            VMEM((SEQ, GROUP * 256), BF16),
            VMEM((SEQ, GROUP * DIM), BF16),
            VMEM((GROUP, 256, SEQ), BF16),
            VMEM((WIDE, GROUP * 256), BF16),
            VMEM((GROUP, 4 * PAIR, PAIR), F32),
            VMEM((GROUP, 4 * WIDE, PAIR), F32),
            VMEM((GROUP, 2, 3, 8, PAIR), F32),
            VMEM((SEQ, GROUP * 256), BF16),
            VMEM((SEQ, 128), F32),
            VMEM((GROUP, 2, 256, PAIR), F32),
            VMEM((LATENT, SEQ), BF16),
            VMEM((WIDE, GROUP * DIM), BF16),
            VMEM((WIDE, GROUP * ROPE), BF16),
            VMEM((LATENT, GROUP * 256), BF16),
            VMEM((SEQ, KEYS), BF16),
            VMEM((4, 2, BLOCK, KEYS), BF16),
            VMEM((4, 2, BLOCK, KEYS), BF16),
            VMEM((2, BLOCK, KEYS), BF16),
            VMEM((2, BLOCK, KEYS), BF16),
            VMEM((2, BLOCK, KEYS), BF16),
            VMEM((2, 2, BLOCK, KEYS), BF16),
            VMEM((2, BLOCK, KEYS), BF16),
            VMEM((2, BLOCK, KEYS), BF16),
            VMEM((4, LATENT, 256), BF16),
            VMEM((LATENT, 256), BF16),
            VMEM((4, 4, 32, 256), BF16),
            VMEM((32, 512), BF16),
            VMEM((32, 512), BF16),
            VMEM((32, 512), BF16),
            VMEM((4, 2, 32, 512), BF16),
            dma(3, 4), dma(3, 4), dma(2), dma(2), dma(2, 2), dma(2, 2), dma(2, 4), dma(2, 4), dma(2), dma(8),
            dma(2), dma(2), dma(2),
            dma(2, 4), dma(2, 4), dma(2, 4), dma(2, 4), dma(2), dma(2), dma(2), dma(2),
            dma(2, 2), dma(2, 2), dma(2), dma(2), dma(2),
            dma(4), dma(4), dma(4, 4), dma(4, 4), dma(2), dma(4, 2), dma(4, 2),
        ],
        compiler_params=pltpu.CompilerParams(collective_id=0, has_side_effects=True, vmem_limit_bytes=58 * MIB),
    )(query_nope[0], query_rope[0], grad_output[0], latent[0], key_rope[0].T, doc_lengths, kv_up)
    anywhere = pl.BlockSpec(memory_space=pl.ANY)
    gqn, gqr, glat, grot, gw = pl.pallas_call(
        finish_kernel,
        name="finish_rows",
        out_shape=[shape(out.shape, out.dtype) for out in outs],
        in_specs=[anywhere] * 5,
        out_specs=[anywhere] * 5,
        scratch_shapes=[VMEM(out.shape, out.dtype) for out in outs] + [dma(2, 5)],
    )(*outs)
    return gqn[None], gqr[None], glat[None], grot.T[None], gw


def solution(mesh):
    rows = P("dp", "ctx", None)
    return jax.shard_map(
        body,
        mesh=mesh,
        in_specs=(rows, rows, rows, rows, rows, P(), P("dp", None)),
        out_specs=(rows, rows, rows, rows, P("ctx", None)),
        check_vma=False,
    )
```

```python
import functools
import math

import jax
import jax.numpy as jnp
from jax import lax
from jax.experimental import pallas as pl
from jax.experimental.pallas import tpu as pltpu
from jax.sharding import PartitionSpec as P

HEADS = 16
DIM = 128
ROPE = 64
LATENT = 512
BLOCK = 128
SEQ = 2048
GROUP = 4
SCALE = (DIM + ROPE) ** -0.5
NEGATIVE = -1e30
MESH = pl.DeviceIdType.MESH
VMEM = pltpu.VMEM
F32 = jnp.float32
BF16 = jnp.bfloat16
MIB = 1 << 20


def coords():
    dp, ctx = lax.axis_index("dp"), lax.axis_index("ctx")
    return dp // 8, (dp // 2) % 4, dp % 2, ctx // 4, ctx % 4


def device(zh, y, c, x, z):
    return ((zh * 4 + y) * 2 + c, x * 4 + z)


def remote(src, dst, send, recv, target):
    return pltpu.make_async_remote_copy(
        src_ref=src, dst_ref=dst, send_sem=send, recv_sem=recv, device_id=target, device_id_type=MESH
    )


def greet(targets):
    barrier = pltpu.get_barrier_semaphore()
    for target in targets:
        pl.semaphore_signal(barrier, inc=1, device_id=target, device_id_type=MESH)
    pl.semaphore_wait(barrier, len(targets))


def dot_bt(left, right):
    return lax.dot_general(left, right, (((1,), (1,)), ((), ())), preferred_element_type=F32)


def dot(left, right):
    return jnp.dot(left, right, preferred_element_type=F32)


PAIR = 2 * BLOCK
WIDE = 4 * BLOCK
KEYS = LATENT + 2 * ROPE


def fold(values, op):
    return op(values.reshape(values.shape[0] // 8, 8, values.shape[1]), axis=0)


def across(a, p):
    return (a % 2 + p % 2) % 2 + 2 * ((a // 2 + p // 2) % 2)


def kernel(
    nope, rope, gout, lat, krope, lens, kv_up,
    o_qn, o_qr, o_lat, o_rot, o_w,
    kblk, w, qn, go, qr, own_lens, other_lens, keys, zstage,
    kx, vx, ktx, qx, st0, st1, stats, dkv, dkr, dqt, latt, dqn, dqr, wp,
    dkp, sin, acc, zin, fin, hin, xin, xsum, zfin, yin, ys, cin, cs, hi_in, fs, ag,
    q_send, q_recv, kx_send, kx_recv, kz_send, kz_recv, ks_send, ks_recv, l_sem, loc,
    zs_sem, kf_send, kf_recv,
    d_send, d_recv, s_send, s_recv, z_send, z_recv, h_send, h_recv, x_send, x_recv, x_loc, zf_send, zf_recv,
    y_send, y_recv, c_send, c_recv, hi_sem, a_send, a_recv,
):
    zh, y, c, x, z = coords()
    s = x // 2
    group = 2 * (x % 2) + c
    sib = device(zh, y, 1 - c, x, z)
    others = [device(zh, y, c, (x + dx) % 4, (z + dz) % 4) for dx in range(4) for dz in range(4) if dx or dz]
    others += [device(zh, y, 1 - c, (x + d) % 4, z) for d in range(4)]
    others += [device(zh, (y + d) % 4, cc, x, z) for d in (1, 2, 3) for cc in (0, 1)]
    others += [device(1 - zh, y, c, x, z)]
    lane = lax.broadcasted_iota(jnp.int32, (1, 2 * ROPE), 1)

    def rows(at, size=BLOCK):
        return pl.ds(pl.multiple_of(at * BLOCK, BLOCK), size)

    def wide_rows(p):
        return pl.ds(pl.multiple_of(p * WIDE, WIDE), WIDE)

    w_copy = pltpu.make_async_copy(kv_up.at[:, pl.ds(pl.multiple_of(group * 1024, 1024), 1024)], w, loc.at[4])
    w_copy.start()
    kblk[:, 0:LATENT] = lat[...]
    pair = krope[...].T
    own_lens[...] = jnp.zeros(own_lens.shape, jnp.int32)
    own_lens[0:1, 0:8] = lens[...]
    kblk[:, LATENT:KEYS] = jnp.concatenate([pair, pair], axis=1)
    greet(others)

    def key_send(t):
        return remote(kblk, keys.at[rows(x)], kx_send.at[t], kx_recv.at[x // 2], device(zh, y, x % 2, 2 * c + t, z))

    def key_local():
        return pltpu.make_async_copy(kblk, keys.at[rows(x)], loc.at[0])

    key_self = [(2 * c + t == x) & (x % 2 == c) for t in (0, 1)]
    for t in (0, 1):
        @pl.when(jnp.logical_not(key_self[t]))
        def _():
            key_send(t).start()

        @pl.when(key_self[t])
        def _():
            key_local().start()

    def zs_copy():
        return remote(kblk, zstage, zs_sem.at[0], zs_sem.at[1], device(zh, y, c, x, across(z, 3)))

    zs_copy().start()

    def q_copies(g, target):
        wide = pl.ds(g * GROUP * DIM, GROUP * DIM)
        thin = pl.ds(g * GROUP * ROPE, GROUP * ROPE)
        return [
            remote(nope.at[:, wide], qn.at[rows(x)], q_send.at[0, g], q_recv.at[0, x], target),
            remote(rope.at[:, thin], qr.at[rows(x)], q_send.at[2, g], q_recv.at[2, x], target),
            remote(gout.at[:, wide], go.at[rows(x)], q_send.at[1, g], q_recv.at[1, x], target),
        ]

    def q_local(g):
        wide = pl.ds(g * GROUP * DIM, GROUP * DIM)
        thin = pl.ds(g * GROUP * ROPE, GROUP * ROPE)
        return [
            pltpu.make_async_copy(nope.at[:, wide], qn.at[rows(x)], loc.at[1]),
            pltpu.make_async_copy(gout.at[:, wide], go.at[rows(x)], loc.at[2]),
            pltpu.make_async_copy(rope.at[:, thin], qr.at[rows(x)], loc.at[3]),
        ]

    q_self = [(2 * c + g // 2 == x) & (c == g % 2) for g in range(4)]
    for g in range(4):
        @pl.when(jnp.logical_not(q_self[g]))
        def _():
            for copy in q_copies(g, device(zh, y, g % 2, 2 * c + g // 2, z)):
                copy.start()

        @pl.when(q_self[g])
        def _():
            for copy in q_local(g):
                copy.start()

    lens_copy = remote(own_lens, other_lens, l_sem.at[0], l_sem.at[1], sib)
    lens_copy.start()

    def key_rows(p, k, core):
        return rows(4 * p + core + 2 * k)

    def z_key(k, p):
        return remote(
            keys.at[key_rows(0, k, c)], keys.at[key_rows(p, k, c)],
            kz_send.at[k, p - 1], kz_recv.at[k, p - 1], device(zh, y, c, x, across(z, p)),
        )

    def kf_copy(t):
        return remote(
            zstage, keys.at[key_rows(3, x // 2, x % 2)],
            kf_send.at[t], kf_recv.at[x // 2], device(zh, y, x % 2, 2 * c + t, z),
        )

    def kf_local():
        return pltpu.make_async_copy(zstage, keys.at[key_rows(3, x // 2, x % 2)], loc.at[0])

    def sib_key(k, p, core):
        at = key_rows(p, k, core)
        return remote(keys.at[at], keys.at[at], ks_send.at[k, p], ks_recv.at[k, p], sib)

    for k in (0, 1):
        own = c + 2 * k
        self_here = (own == x) & (s == c)

        @pl.when(jnp.logical_not(self_here))
        def _():
            remote(kblk, keys.at[rows(own)], kx_send.at[0], kx_recv.at[k], sib).wait_recv()

        @pl.when(self_here)
        def _():
            key_local().wait()

        for p in (1, 2):
            z_key(k, p).start()
        sib_key(k, 0, c).start()

    def take(p):
        for k in (0, 1):
            sib_key(k, p, 1 - c).wait_recv()

    def pass_on(p):
        for k in (0, 1):
            z_key(k, p).wait_recv()
            sib_key(k, p, c).start()

    def pass_last():
        for k in (0, 1):
            self_here = (c + 2 * k == x) & (s == c)

            @pl.when(jnp.logical_not(self_here))
            def _():
                remote(zstage, keys.at[key_rows(3, k, c)], kf_send.at[0], kf_recv.at[k], sib).wait_recv()

            @pl.when(self_here)
            def _():
                kf_local().wait()

            sib_key(k, 3, c).start()

    w_copy.wait()
    wt = [w[:, h * 256:h * 256 + DIM].T for h in range(GROUP)]

    def project(p):
        at = wide_rows(p)
        own = keys[at, 0:LATENT]
        rot = keys[at, LATENT:KEYS]
        rot_t = rot.T
        for h in range(GROUP):
            both = dot(own, w[:, h * 256:(h + 1) * 256]).astype(BF16)
            kx[at, h * 256:h * 256 + DIM] = both[:, 0:DIM]
            kx[at, h * 256 + DIM:(h + 1) * 256] = rot
            vx[at, h * DIM:(h + 1) * DIM] = both[:, DIM:256]
            ktx[h, 0:DIM, at] = dot_bt(wt[h], own).astype(BF16)
            ktx[h, DIM:256, at] = rot_t
        latt[:, at] = own.T

    def first(p, carry):
        @pl.when(p == 1)
        def _():
            zs_copy().wait_recv()
            for t in (0, 1):
                @pl.when(jnp.logical_not(key_self[t]))
                def _():
                    kf_copy(t).start()

                @pl.when(key_self[t])
                def _():
                    kf_local().start()
            pass_on(1)

        take(p)
        project(p)
        return carry

    lax.fori_loop(0, 2, first, 0)

    lens_copy.wait_recv()
    sizes = jnp.where(s == c, own_lens[0:1, :], other_lens[0:1, :])
    row_lane = lax.broadcasted_iota(jnp.int32, (1, PAIR), 1)
    positions, starts = [], []
    for t in (0, 1):
        pos = (4 * (2 * t + row_lane // BLOCK) + z) * BLOCK + row_lane % BLOCK
        start = jnp.zeros_like(pos)
        end = jnp.zeros_like(sizes[:, 0:1])
        for d in range(8):
            end = end + sizes[:, d:d + 1]
            start = jnp.maximum(start, jnp.where(end <= pos, end, 0))
        positions.append(pos)
        starts.append(start)
    stats[...] = jnp.zeros(stats.shape, F32)
    for h in range(GROUP):
        for t in (0, 1):
            stats[h, t, 0] = jnp.full((8, PAIR), NEGATIVE, F32)
    dqt[...] = jnp.zeros(dqt.shape, F32)

    for xs in range(4):
        self_here = (xs == x) & (s == c)

        @pl.when(jnp.logical_not(self_here))
        def _():
            at = rows(xs)
            remote(nope.at[:, 0:GROUP * DIM], qn.at[at], q_send.at[0, 0], q_recv.at[0, xs], sib).wait_recv()
            remote(rope.at[:, 0:GROUP * ROPE], qr.at[at], q_send.at[2, 0], q_recv.at[2, xs], sib).wait_recv()
            remote(gout.at[:, 0:GROUP * DIM], go.at[at], q_send.at[1, 0], q_recv.at[1, xs], sib).wait_recv()
    for g in range(4):
        @pl.when(q_self[g])
        def _():
            for copy in q_local(g):
                copy.wait()
    for h in range(GROUP):
        qx[:, h * 256:h * 256 + DIM] = qn[:, h * DIM:(h + 1) * DIM]
        half = qr[:, (h // 2) * 128:(h // 2) * 128 + 128]
        keep = (lane < ROPE) if h % 2 == 0 else (lane >= ROPE)
        qx[:, h * 256 + DIM:(h + 1) * 256] = jnp.where(keep, half, jnp.zeros_like(half))

    pairs = [slice(0, PAIR), slice(PAIR, WIDE)]
    spans = [PAIR, WIDE]
    scores = [st0, st1]

    def span(p, t):
        return pl.ds(pl.multiple_of(p * spans[t], spans[t]), spans[t])

    def key_span(p, t):
        return pl.ds(pl.multiple_of(p * WIDE, WIDE), spans[t])

    def look(p):
        base = lax.broadcasted_iota(jnp.int32, (WIDE, 1), 0)
        key = base + (base // BLOCK) * (3 * BLOCK) + across(z, p) * BLOCK
        for t in (0, 1):
            part = key[0:spans[t]]
            seen = (part <= positions[t]) & (part >= starts[t])
            for h in range(GROUP):
                at = key_span(p, t)
                v = dot_bt(kx[at, h * 256:(h + 1) * 256], qx[pairs[t], h * 256:(h + 1) * 256])
                d = dot_bt(vx[at, h * DIM:(h + 1) * DIM], go[pairs[t], h * DIM:(h + 1) * DIM])
                v = jnp.where(seen, v * (SCALE * math.log2(math.e)), NEGATIVE)
                scores[t][h, span(p, t), :] = v
                old = stats[h, t, 0]
                top = jnp.maximum(old, fold(v, jnp.max))
                e = jnp.exp2(v.reshape(spans[t] // 8, 8, PAIR) - top[None])
                factor = jnp.exp2(old - top)
                stats[h, t, 0] = top
                stats[h, t, 1] = stats[h, t, 1] * factor + jnp.sum(e, axis=0)
                stats[h, t, 2] = stats[h, t, 2] * factor + jnp.sum(e * d.reshape(spans[t] // 8, 8, PAIR), axis=0)

    def early(p, carry):
        look(p)

        @pl.when(p == 0)
        def _():
            pass_on(2)

        return carry

    def late(p, carry):
        take(p)
        project(p)

        @pl.when(p == 2)
        def _():
            pass_last()

        look(p)
        return carry

    lax.fori_loop(0, 2, early, 0)
    lax.fori_loop(2, 4, late, 0)

    logs, inners = [], []
    for h in range(GROUP):
        for t in (0, 1):
            top8 = stats[h, t, 0]
            top = jnp.max(top8, axis=0, keepdims=True)
            factor = jnp.exp2(top8 - top)
            total = jnp.sum(stats[h, t, 1] * factor, axis=0, keepdims=True)
            inners.append(jnp.sum(stats[h, t, 2] * factor, axis=0, keepdims=True) / total)
            logs.append(top + jnp.log2(total))

    def grads(p):
        at = wide_rows(p)
        low = pl.ds(pl.multiple_of(p * WIDE, WIDE), PAIR)
        high = pl.ds(pl.multiple_of(p * WIDE + PAIR, PAIR), PAIR)
        rot_low = jnp.zeros((PAIR, 2 * ROPE), F32)
        rot_high = jnp.zeros((PAIR, 2 * ROPE), F32)
        for h in range(GROUP):
            probs, diffs = [], []
            for t in (0, 1):
                e = jnp.exp2(scores[t][h, span(p, t), :] - logs[2 * h + t])
                d = dot_bt(vx[key_span(p, t), h * DIM:(h + 1) * DIM], go[pairs[t], h * DIM:(h + 1) * DIM])
                diff = (e * (d - inners[2 * h + t])).astype(BF16)
                dqt[h, t] += dot(ktx[h, :, key_span(p, t)], diff)
                probs.append(e.astype(BF16))
                diffs.append(diff)
            q_at, g_at = slice(h * 256, (h + 1) * 256), slice(h * DIM, (h + 1) * DIM)
            dk = SCALE * dot(jnp.concatenate([diffs[0], diffs[1][0:PAIR]], axis=1), qx[:, q_at])
            dv = dot(jnp.concatenate([probs[0], probs[1][0:PAIR]], axis=1), go[:, g_at])
            dkv[low, h * 256:h * 256 + DIM] = dk[:, 0:DIM].astype(BF16)
            dkv[low, h * 256 + DIM:(h + 1) * 256] = dv.astype(BF16)
            rot_low = rot_low + dk[:, DIM:256]
            dk = SCALE * dot(diffs[1][PAIR:WIDE], qx[pairs[1], q_at])
            dv = dot(probs[1][PAIR:WIDE], go[pairs[1], g_at])
            dkv[high, h * 256:h * 256 + DIM] = dk[:, 0:DIM].astype(BF16)
            dkv[high, h * 256 + DIM:(h + 1) * 256] = dv.astype(BF16)
            rot_high = rot_high + dk[:, DIM:256]
        dkr[low, :] = rot_low
        dkr[high, :] = rot_high

    def d_places():
        wide = pl.ds(pl.multiple_of(group * 512, 512), 512)
        thin = pl.ds(pl.multiple_of(group * 256, 256), 256)
        return o_qn.at[:, wide], o_qr.at[:, thin]

    def d_copies(xs):
        target = device(zh, y, s, xs, z)
        at = rows(xs)
        wide, thin = d_places()
        return [
            remote(dqn.at[at], wide, d_send.at[0, xs], d_recv.at[0, group], target),
            remote(dqr.at[at], thin, d_send.at[1, xs], d_recv.at[1, group], target),
        ]

    def d_local():
        at = rows(x)
        wide, thin = d_places()
        return [
            pltpu.make_async_copy(dqn.at[at], wide, loc.at[5]),
            pltpu.make_async_copy(dqr.at[at], thin, loc.at[6]),
        ]

    d_self = [(xs == x) & (s == c) for xs in range(4)]

    def send_queries():
        for t in (0, 1):
            rots = []
            for h in range(GROUP):
                dq = SCALE * dqt[h, t].T
                dqn[pairs[t], h * DIM:(h + 1) * DIM] = dq[:, 0:DIM].astype(BF16)
                rots.append(dq[:, DIM:256])
            for half in (0, 1):
                both = jnp.where(lane < ROPE, rots[2 * half], rots[2 * half + 1])
                dqr[pairs[t], half * 128:(half + 1) * 128] = both.astype(BF16)
        for xs in range(4):
            @pl.when(jnp.logical_not(d_self[xs]))
            def _():
                for copy in d_copies(xs):
                    copy.start()

            @pl.when(d_self[xs])
            def _():
                for copy in d_local():
                    copy.start()

    def y_copy(d):
        peer = (y + d) % 4
        return remote(
            wp.at[:, pl.ds(pl.multiple_of(peer * 256, 256), 256)], yin.at[d - 1],
            y_send.at[d - 1], y_recv.at[d - 1], device(zh, peer, c, x, z),
        )

    def send_weights():
        for d in (2, 1, 3, 0):
            at = pl.ds(pl.multiple_of(((y + d) % 4) * 256, 256), 256)
            wp[:, at] = dot(latt[...], dkv[:, at]).astype(BF16)
            if d > 0:
                y_copy(d).start()

    def s_copy(k, p):
        return remote(dkp.at[key_rows(p, k, 1 - c)], sin.at[p, k], s_send.at[k, p], s_recv.at[k, p], sib)

    def z_copy(k):
        return remote(acc.at[1, k], zin.at[k], z_send.at[k], z_recv.at[k], device(zh, y, c, x, across(z, 1)))

    def x_copy(k, p):
        return remote(
            acc.at[p, k], xin.at[p - 2, x % 2],
            x_send.at[k, p - 2], x_recv.at[x % 2, p - 2], device(zh, y, s, c + 2 * k, z),
        )

    def x_local(k, p):
        return pltpu.make_async_copy(acc.at[p, k], xin.at[p - 2, x % 2], x_loc.at[p - 2])

    h_self = [(c + 2 * k == x) & (s == c) for k in (0, 1)]

    def join(p):
        for k in (0, 1):
            s_copy(k, p).wait_recv()
            acc[p, k] = (dkp[key_rows(p, k, c), :].astype(F32) + sin[p, k].astype(F32)).astype(BF16)

    def send_join(p):
        for k in (0, 1):
            @pl.when(jnp.logical_not(h_self[k]))
            def _():
                x_copy(k, p).start()

            @pl.when(h_self[k])
            def _():
                x_local(k, p).start()

    def back(q, carry):
        p = 3 - q
        grads(p)
        at = wide_rows(p)
        dkp[at, 0:LATENT] = dot_bt(dkv[at, :], w[...]).astype(BF16)
        rot = dkr[at, :]
        dkp[at, LATENT:KEYS] = (rot + pltpu.roll(rot, ROPE, 1)).astype(BF16)
        for k in (0, 1):
            s_copy(k, p).start()

        @pl.when(q > 0)
        def _():
            join(p + 1)

        @pl.when((q == 1) | (q == 2))
        def _():
            send_join(p + 1)

        @pl.when(q == 3)
        def _():
            for k in (0, 1):
                z_copy(k).start()
        return carry

    lax.fori_loop(0, 4, back, 0)
    send_weights()
    join(0)

    def zf_copy(p):
        return remote(xsum.at[p - 2], zfin.at[p - 2], zf_send.at[p - 2], zf_recv.at[p - 2], device(zh, y, c, x, across(z, p)))

    for p in (3, 2):
        for t in (0, 1):
            self_here = (2 * c + t == x) & (x % 2 == c)

            @pl.when(jnp.logical_not(self_here))
            def _():
                remote(acc.at[p, 0], xin.at[p - 2, t], x_send.at[0, p - 2], x_recv.at[t, p - 2], sib).wait_recv()

            @pl.when(self_here)
            def _():
                x_local(0, p).wait()
        xsum[p - 2] = (xin[p - 2, 0].astype(F32) + xin[p - 2, 1].astype(F32)).astype(BF16)
        zf_copy(p).start()

    send_queries()

    for d in (1, 3, 2):
        y_copy(d).wait_recv()
    mine = wp[:, pl.ds(pl.multiple_of(y * 256, 256), 256)].astype(F32)
    ys[...] = (mine + yin[0].astype(F32) + yin[1].astype(F32) + yin[2].astype(F32)).astype(BF16)

    def c_copy(dx, dz):
        px, pz = (x + dx) % 4, (z + dz) % 4
        src = ys.at[pl.ds(pl.multiple_of((4 * px + pz) * 32, 32), 32)]
        return remote(src, cin.at[dx, dz], c_send.at[dx, dz], c_recv.at[dx, dz], device(zh, y, c, px, pz))

    mates = [(dx, dz) for dz in (2, 1, 3, 0) for dx in (2, 1, 3, 0) if dx or dz]
    for dx, dz in mates:
        c_copy(dx, dz).start()

    def h_copy(k):
        return remote(fin.at[k], hin.at[x % 2], h_send.at[k], h_recv.at[x % 2], device(zh, y, s, c + 2 * k, z))

    def h_local(k):
        return pltpu.make_async_copy(fin.at[k], hin.at[x % 2], loc.at[7])

    for k in (0, 1):
        z_copy(k).wait_recv()
        total = acc[0, k].astype(F32) + zin[k].astype(F32)
        fin[k] = total.astype(BF16)

        @pl.when(jnp.logical_not(h_self[k]))
        def _():
            h_copy(k).start()

        @pl.when(h_self[k])
        def _():
            h_local(k).start()

    for dx, dz in mates:
        c_copy(dx, dz).wait_recv()
    own = ys[pl.ds(pl.multiple_of((4 * x + z) * 32, 32), 32), :].astype(F32)
    even = own
    for dz in (1, 2, 3):
        even = even + cin[0, dz].astype(F32)
    for dz in range(4):
        even = even + cin[2, dz].astype(F32)
    odd = jnp.zeros_like(own)
    for dx in (1, 3):
        for dz in range(4):
            odd = odd + cin[dx, dz].astype(F32)
    flip = x % 2 == 1
    cs[:, 0:256] = jnp.where(flip, odd, even).astype(BF16)
    cs[:, 256:512] = jnp.where(flip, even, odd).astype(BF16)
    hi_copy = remote(cs, hi_in, hi_sem.at[0], hi_sem.at[1], device(1 - zh, y, c, x, z))
    hi_copy.start()

    for t in (0, 1):
        self_here = (2 * c + t == x) & (x % 2 == c)

        @pl.when(jnp.logical_not(self_here))
        def _():
            remote(fin.at[0], hin.at[t], h_send.at[0], h_recv.at[t], sib).wait_recv()
    for k in (0, 1):
        @pl.when(h_self[k])
        def _():
            h_local(k).wait()
    final = hin[0].astype(F32) + hin[1].astype(F32)
    for p in (3, 2):
        zf_copy(p).wait_recv()
        final = final + zfin[p - 2].astype(F32)
    o_lat[...] = final[:, 0:LATENT].astype(BF16)
    o_rot[...] = final[:, LATENT:KEYS].T[0:ROPE, :].astype(BF16)

    hi_copy.wait_recv()
    fs[...] = (cs[...].astype(F32) + hi_in[...].astype(F32)).astype(BF16)

    def a_copy(dy, dc):
        peer = device(zh, (y + dy) % 4, (c + dc) % 2, x, z)
        return remote(fs, ag.at[dy, dc], a_send.at[dy, dc], a_recv.at[dy, dc], peer)

    members = [(dy, dc) for dy in (2, 1, 3, 0) for dc in (0, 1) if dy or dc]
    for dy, dc in members:
        a_copy(dy, dc).start()

    def place(values, from_y, from_c):
        wide = values.astype(F32)
        for parity in (0, 1):
            at = pl.multiple_of((2 * parity + from_c) * 1024 + from_y * 256, 256)
            o_w[:, pl.ds(at, 256)] = wide[:, parity * 256:(parity + 1) * 256]

    place(fs[...], y, c)
    for dy, dc in members:
        a_copy(dy, dc).wait_recv()
        place(ag[dy, dc], (y + 4 - dy) % 4, (c + dc) % 2)

    for gs in range(4):
        self_here = (group == gs) & (s == c)

        @pl.when(jnp.logical_not(self_here))
        def _():
            remote(dqn.at[0:BLOCK], o_qn.at[:, gs * 512:(gs + 1) * 512], d_send.at[0, 0], d_recv.at[0, gs], sib).wait_recv()
            remote(dqr.at[0:BLOCK], o_qr.at[:, gs * 256:(gs + 1) * 256], d_send.at[1, 0], d_recv.at[1, gs], sib).wait_recv()

    for t in (0, 1):
        @pl.when(jnp.logical_not(key_self[t]))
        def _():
            key_send(t).wait_send()
    for g in range(4):
        @pl.when(jnp.logical_not(q_self[g]))
        def _():
            for copy in q_copies(g, sib):
                copy.wait_send()
    lens_copy.wait_send()
    for k in (0, 1):
        for p in (1, 2):
            z_key(k, p).wait_send()
        z_copy(k).wait_send()
        for p in range(4):
            sib_key(k, p, c).wait_send()
            s_copy(k, p).wait_send()

        @pl.when(jnp.logical_not(h_self[k]))
        def _():
            h_copy(k).wait_send()
    zs_copy().wait_send()
    for t in (0, 1):
        @pl.when(jnp.logical_not(key_self[t]))
        def _():
            kf_copy(t).wait_send()
    for p in (3, 2):
        zf_copy(p).wait_send()
        for k in (0, 1):
            @pl.when(jnp.logical_not(h_self[k]))
            def _():
                x_copy(k, p).wait_send()
    for xs in range(4):
        @pl.when(jnp.logical_not(d_self[xs]))
        def _():
            for copy in d_copies(xs):
                copy.wait_send()

        @pl.when(d_self[xs])
        def _():
            for copy in d_local():
                copy.wait()
    for d in (1, 2, 3):
        y_copy(d).wait_send()
    for dx, dz in mates:
        c_copy(dx, dz).wait_send()
    hi_copy.wait_send()
    for dy, dc in members:
        a_copy(dy, dc).wait_send()


def shape(dims, kind=BF16):
    return jax.ShapeDtypeStruct(dims, kind)


def dma(*dims):
    return pltpu.SemaphoreType.DMA(dims)


def finish_kernel(*refs):
    sems = refs[15]
    into = [pltpu.make_async_copy(refs[i], refs[10 + i], sems.at[0, i]) for i in range(5)]
    out = [pltpu.make_async_copy(refs[10 + i], refs[5 + i], sems.at[1, i]) for i in range(5)]
    for copy in into:
        copy.start()
    for i in range(5):
        into[i].wait()
        out[i].start()
    for copy in out:
        copy.wait()


def body(query_nope, query_rope, latent, key_rope, grad_output, kv_up, doc_lengths):
    here = pl.BlockSpec(memory_space=pltpu.VMEM)
    outs = pl.pallas_call(
        kernel,
        name="whole_rows",
        out_shape=(
            shape((BLOCK, HEADS * DIM)),
            shape((BLOCK, HEADS * ROPE)),
            shape((BLOCK, LATENT)),
            shape((ROPE, BLOCK)),
            shape((32, HEADS * 256), F32),
        ),
        in_specs=[here] * 6 + [pl.BlockSpec(memory_space=pl.ANY)],
        out_specs=(here,) * 5,
        scratch_shapes=[
            VMEM((BLOCK, KEYS), BF16),
            VMEM((LATENT, GROUP * 256), BF16),
            VMEM((WIDE, GROUP * DIM), BF16),
            VMEM((WIDE, GROUP * DIM), BF16),
            VMEM((WIDE, GROUP * ROPE), BF16),
            VMEM((8, 128), jnp.int32),
            VMEM((8, 128), jnp.int32),
            VMEM((SEQ, KEYS), BF16),
            VMEM((BLOCK, KEYS), BF16),
            VMEM((SEQ, GROUP * 256), BF16),
            VMEM((SEQ, GROUP * DIM), BF16),
            VMEM((GROUP, 256, SEQ), BF16),
            VMEM((WIDE, GROUP * 256), BF16),
            VMEM((GROUP, 4 * PAIR, PAIR), F32),
            VMEM((GROUP, 4 * WIDE, PAIR), F32),
            VMEM((GROUP, 2, 3, 8, PAIR), F32),
            VMEM((SEQ, GROUP * 256), BF16),
            VMEM((SEQ, 128), F32),
            VMEM((GROUP, 2, 256, PAIR), F32),
            VMEM((LATENT, SEQ), BF16),
            VMEM((WIDE, GROUP * DIM), BF16),
            VMEM((WIDE, GROUP * ROPE), BF16),
            VMEM((LATENT, GROUP * 256), BF16),
            VMEM((SEQ, KEYS), BF16),
            VMEM((4, 2, BLOCK, KEYS), BF16),
            VMEM((4, 2, BLOCK, KEYS), BF16),
            VMEM((2, BLOCK, KEYS), BF16),
            VMEM((2, BLOCK, KEYS), BF16),
            VMEM((2, BLOCK, KEYS), BF16),
            VMEM((2, 2, BLOCK, KEYS), BF16),
            VMEM((2, BLOCK, KEYS), BF16),
            VMEM((2, BLOCK, KEYS), BF16),
            VMEM((4, LATENT, 256), BF16),
            VMEM((LATENT, 256), BF16),
            VMEM((4, 4, 32, 256), BF16),
            VMEM((32, 512), BF16),
            VMEM((32, 512), BF16),
            VMEM((32, 512), BF16),
            VMEM((4, 2, 32, 512), BF16),
            dma(3, 4), dma(3, 4), dma(2), dma(2), dma(2, 2), dma(2, 2), dma(2, 4), dma(2, 4), dma(2), dma(8),
            dma(2), dma(2), dma(2),
            dma(2, 4), dma(2, 4), dma(2, 4), dma(2, 4), dma(2), dma(2), dma(2), dma(2),
            dma(2, 2), dma(2, 2), dma(2), dma(2), dma(2),
            dma(4), dma(4), dma(4, 4), dma(4, 4), dma(2), dma(4, 2), dma(4, 2),
        ],
        compiler_params=pltpu.CompilerParams(collective_id=0, has_side_effects=True, vmem_limit_bytes=58 * MIB),
    )(query_nope[0], query_rope[0], grad_output[0], latent[0], key_rope[0].T, doc_lengths, kv_up)
    anywhere = pl.BlockSpec(memory_space=pl.ANY)
    gqn, gqr, glat, grot, gw = pl.pallas_call(
        finish_kernel,
        name="finish_rows",
        out_shape=[shape(out.shape, out.dtype) for out in outs],
        in_specs=[anywhere] * 5,
        out_specs=[anywhere] * 5,
        scratch_shapes=[VMEM(out.shape, out.dtype) for out in outs] + [dma(2, 5)],
    )(*outs)
    return gqn[None], gqr[None], glat[None], grot.T[None], gw


def solution(mesh):
    rows = P("dp", "ctx", None)
    return jax.shard_map(
        body,
        mesh=mesh,
        in_specs=(rows, rows, rows, rows, rows, P(), P("dp", None)),
        out_specs=(rows, rows, rows, rows, P("ctx", None)),
        check_vma=False,
    )
```
